32 devices in a mesh: stream: 2 (over x), span: 4 (over y, core), depth: 4 (over z).
Axes of the slice: x: 2, y: 2, z: 4, core: 2. Of those that a mesh axis runs over, the one named last changes fastest.
Arguments:
- forward_velocity: float32 [3, 16, 64, 512], P(None, 'stream', 'span', 'depth'), may hold values from -40 to 40, as said below
- adjoint_velocity: float32 [3, 16, 64, 512], P(None, 'stream', 'span', 'depth'), may hold values from -40 to 40, as said below
- weights: float32 [32, 81], replicated, may hold values from -0.625 to 0.625
Outputs:
- basis: float32 [32, 16, 64, 512], P(None, 'stream', 'span', 'depth')
The draws below stay inside these ranges and needn't reach their ends.
Inputs may be any that keep to these rules, and one draw needn't show every extreme that they name: `forward_velocity`: a velocity field whose amplitude varies from cell to cell. `adjoint_velocity`: a velocity field whose amplitude varies from cell to cell.
All inputs are finite; a program needn't handle non-finite values.
Results may differ from the reference program's by a relative error of at most 0.0003.
Values sent between devices are 32-bit elements; how exact they have to be, the bound alone decides.
A program may use at most 64 MiB of HBM per device.

```python
import jax
import jax.numpy as jnp
from jax import lax

CX = 8
NSNAP = 32
PAIRS = 81
NX = 16
NY = 64
NZ = 512
CELLS = 524288


def velocity_field(key):
    base_key, scale_key = jax.random.split(key)
    shape = (3, NX, NY, NZ)
    unit = jax.random.uniform(scale_key, (1, NX, NY, NZ), jnp.float32)
    pos_x = jnp.arange(NX, dtype=jnp.float32)[:, None, None] / NX
    pos_y = jnp.arange(NY, dtype=jnp.float32)[None, :, None] / NY
    pos_z = jnp.arange(NZ, dtype=jnp.float32)[None, None, :] / NZ
    position = (pos_x + pos_y + pos_z)[None]
    values = jnp.clip(jax.random.normal(base_key, shape, jnp.float32), -4.0, 4.0)
    amplitude = jnp.exp(jnp.log(10.0) * unit - 1.15) * jnp.exp(0.25 * jnp.log(3.0) * position)
    return (values * amplitude).astype(jnp.float32)


def draw_forward_velocity(key, part):
    return velocity_field(jax.random.fold_in(key, 101))


def draw_adjoint_velocity(key, part):
    return velocity_field(jax.random.fold_in(key, 202))


def normal_values(stream_key, dims, width, most, kind=jnp.bfloat16):
    array = jax.random.normal(stream_key, dims, jnp.float32) * width
    return jnp.minimum(jnp.maximum(array, -most), most).astype(kind)


def setup_inputs(seed: int = 0) -> dict:
    key_of = jax.random.split(jax.random.key(seed), 4)
    forward_velocity = draw_forward_velocity(jax.random.fold_in(key_of[3], 71), 0)
    adjoint_velocity = draw_adjoint_velocity(jax.random.fold_in(key_of[3], 71), 0)
    weights = normal_values(key_of[2], (NSNAP, PAIRS), PAIRS ** -0.5, 0.625, jnp.float32)
    return dict(forward_velocity=forward_velocity, adjoint_velocity=adjoint_velocity, weights=weights)


def shifted(field, axis, offset):
    parts = [slice(None), slice(2, -2), slice(2, -2), slice(2, -2)]
    length = field.shape[axis]
    parts[axis] = slice(2 + offset, length - 2 + offset)
    return field[tuple(parts)]

def gradients(padded):
    slopes = []
    for axis in (1, 2, 3):
        near = shifted(padded, axis, 1) - shifted(padded, axis, -1)
        far = shifted(padded, axis, 2) - shifted(padded, axis, -2)
        slopes.append((8.0 * near - far) / 12.0)
    stacked = jnp.stack(slopes, axis=1)
    return stacked.reshape(stacked.shape[0] * 3, -1)

def snapshots(padded, weights):
    grads = gradients(padded)
    products = (grads[:9][:, None, :] * grads[9:][None, :, :]).reshape(81, -1)
    return jnp.dot(weights.astype(jnp.float32), products.astype(jnp.float32), precision=lax.Precision.HIGHEST, preferred_element_type=jnp.float32)

def reference(forward_velocity, adjoint_velocity, weights):
    stacked = jnp.concatenate([forward_velocity, adjoint_velocity], 0)
    padded = jnp.pad(stacked, ((0, 0), (2, 2), (2, 2), (2, 2)), mode='wrap')
    blocks = NX // CX

    def one_block(index):
        start = (index * CX).astype(jnp.int32)
        piece = lax.dynamic_slice_in_dim(padded, start, CX + 4, 1)
        return snapshots(piece, weights)
    snaps = lax.map(one_block, jnp.arange(blocks, dtype=jnp.int32))

    def block_gram(block):
        return jnp.dot(block.astype(jnp.float32), block.T.astype(jnp.float32), precision=lax.Precision.HIGHEST, preferred_element_type=jnp.float32)
    gram = jnp.sum(lax.map(block_gram, snaps), axis=0)
    lower = jnp.linalg.cholesky(gram / CELLS)
    inverse = jax.scipy.linalg.solve_triangular(lower, jnp.eye(NSNAP, dtype=jnp.float32), lower=True)

    def block_basis(block):
        return jnp.dot(inverse.astype(jnp.float32), block.astype(jnp.float32), precision=lax.Precision.HIGHEST, preferred_element_type=jnp.float32)
    basis = lax.map(block_basis, snaps)
    basis = basis.reshape(blocks, NSNAP, CX, NY, NZ).transpose(1, 0, 2, 3, 4)
    return basis.reshape(NSNAP, NX, NY, NZ)
```

```python
import functools

import jax
import jax.numpy as jnp
from jax import lax
from jax.experimental import pallas as pl
from jax.experimental.pallas import tpu as pltpu
from jax.sharding import PartitionSpec as P

MESH = pl.DeviceIdType.MESH
F32 = jnp.float32
BF16 = jnp.bfloat16
AXES = ("stream", "span", "depth")
VMEM = pl.BlockSpec(memory_space=pltpu.VMEM)
LIMIT = 48 * 1024 * 1024


def halo_kernel(sizes, f_ref, a_ref, hx, hy, hz, ysend, zsend, send, recv):
    ids = [lax.axis_index(name) for name in AXES]
    peers = []
    for name, size, me in zip(AXES, sizes, ids):
        peers.append({name: lax.rem(me + 1, size)})
        peers.append({name: lax.rem(me + size - 1, size)})
    barrier = pltpu.get_barrier_semaphore()
    for peer in peers:
        pl.semaphore_signal(barrier, inc=1, device_id=peer, device_id_type=MESH)

    planes, rows = f_ref.shape[1], f_ref.shape[2]
    half = 3 * planes
    for k, ref in enumerate((f_ref, a_ref)):
        flat = ref.reshape(half * rows, 128)
        for j in range(2):
            ysend[0, j, k * half:(k + 1) * half, :] = flat[pl.ds(rows - 2 + j, half, stride=rows), :]
            ysend[1, j, k * half:(k + 1) * half, :] = flat[pl.ds(j, half, stride=rows), :]

    pl.semaphore_wait(barrier, len(peers))
    copies = []

    def push(src, dst, peer):
        n = len(copies)
        copy = pltpu.make_async_remote_copy(
            src_ref=src, dst_ref=dst, send_sem=send.at[n], recv_sem=recv.at[n],
            device_id=peer, device_id_type=MESH)
        copy.start()
        copies.append(copy)

    for k, ref in enumerate((f_ref, a_ref)):
        push(ref.at[:, planes - 2:planes], hx.at[0, 3 * k:3 * k + 3], peers[0])
        push(ref.at[:, 0:2], hx.at[1, 3 * k:3 * k + 3], peers[1])
    push(ysend.at[0], hy.at[0], peers[2])
    push(ysend.at[1], hy.at[1], peers[3])

    lane = lax.broadcasted_iota(jnp.int32, (rows, 128), 1)
    for k, ref in enumerate((f_ref, a_ref)):
        last = jnp.zeros((rows, 128), F32)
        first = jnp.zeros((rows, 128), F32)
        for c in range(3):
            for x in range(planes):
                i = c * planes + x
                own = ref[c, x]
                head = jnp.where(lane == 0, -own, 8.0 * pltpu.roll(own, 1, 1) - own)
                tail = jnp.where(lane == 126, own - 8.0 * pltpu.roll(own, 127, 1), own)
                head = pltpu.roll(head, 4 * i, 1) if i else head
                tail = pltpu.roll(tail, (4 * i + 4) % 128, 1)
                first = jnp.where(lane // 4 == i, head, first)
                last = jnp.where(lane // 4 == i, tail, last)
        zsend[0, k] = last
        zsend[1, k] = first
    push(zsend.at[0], hz.at[0], peers[4])
    push(zsend.at[1], hz.at[1], peers[5])
    for copy in copies:
        copy.wait()


def split(value):
    high = value.astype(BF16)
    low = (value - high.astype(F32)).astype(BF16)
    return high, low


def snap_kernel(f_ref, a_ref, hx, hy, hz, w_ref, s_ref, g_ref, px, py, gs, rhs, lhs, acc):
    planes, rows = f_ref.shape[1], f_ref.shape[2]
    half = 3 * planes
    cells = rows * 128
    row = lax.broadcasted_iota(jnp.int32, (81, 176), 0)
    col = lax.broadcasted_iota(jnp.int32, (81, 176), 1)
    block, r = col // 16, col % 8
    source = jnp.where(block < 9, block * 9 + r, jnp.where(block == 9, r * 9 + 8, 80))
    keep = (row == source) & ((block < 10) | (r == 0))
    pick = jnp.where(keep, 1.0, 0.0).astype(BF16)
    w_high, w_low = split(w_ref[...] * (1.0 / 144.0))
    lhs[0:32, :] = jnp.dot(w_high, pick, preferred_element_type=F32).astype(BF16)
    lhs[32:64, :] = jnp.dot(w_low, pick, preferred_element_type=F32).astype(BF16)

    for k, ref in enumerate((f_ref, a_ref)):
        px[3 * k:3 * k + 3, 2:planes + 2] = ref[...]
        for c in range(3):
            py[(3 * k + c) * planes:(3 * k + c + 1) * planes, 8:8 + rows, :] = ref[c]
    px[:, 0:2] = hx[0]
    px[:, planes + 2:planes + 4] = hx[1]
    flat = py.reshape(2 * half * (rows + 16), 128)
    for j in range(2):
        flat[pl.ds(6 + j, 2 * half, stride=rows + 16), :] = hy[0, j]
        flat[pl.ds(8 + rows + j, 2 * half, stride=rows + 16), :] = hy[1, j]

    lane = lax.broadcasted_iota(jnp.int32, (rows, 128), 1)
    acc[...] = jnp.zeros_like(acc)

    def stencil(m2, m1, p1, p2):
        return 8.0 * (p1 - m1) - (p2 - m2)

    @pl.loop(0, planes)
    def _(x):
        for k in range(2):
            halo_z = jnp.where(lane % 4 < 2, hz[1, k], hz[0, k])
            for c in range(3):
                m = 3 * k + c
                own = px[m, x + 2]
                dx = stencil(px[m, x], px[m, x + 1], px[m, x + 3], px[m, x + 4])
                i = m * planes + x
                dy = stencil(*[py[i, 8 + o:8 + o + rows, :] for o in (-2, -1, 1, 2)])
                p1 = jnp.where(lane == 127, 0.0, pltpu.roll(own, 127, 1))
                p2 = jnp.where(lane >= 126, 0.0, pltpu.roll(own, 126, 1))
                m1 = jnp.where(lane == 0, 0.0, pltpu.roll(own, 1, 1))
                m2 = jnp.where(lane <= 1, 0.0, pltpu.roll(own, 2, 1))
                edge = pltpu.roll(halo_z, lax.rem(254 - 4 * (c * planes + x), 128), 1)
                dz = stencil(m2, m1, p1, p2) + jnp.where((lane < 2) | (lane >= 126), edge, 0.0)
                for d, slope in enumerate((dx, dy, dz)):
                    gs[pl.ds(16 * k + 3 * c + d, rows, stride=32), :] = slope
        for y in range(rows):
            base = 32 * y
            f8 = gs[base:base + 8, :]
            a8 = gs[base + 16:base + 24, :]
            a_end = gs[base + 24:base + 25, :]
            for n in range(11):
                if n < 9:
                    part = gs[base + n:base + n + 1, :] * a8
                elif n == 9:
                    part = f8 * a_end
                else:
                    part = jnp.broadcast_to(gs[base + 8:base + 9, :] * a_end, (8, 128))
                high = part.astype(BF16).astype(F32)
                both = jnp.concatenate([high, part - high], axis=0).astype(BF16)
                rhs[16 * n:16 * n + 16, 128 * y:128 * y + 128] = both
        wide = jnp.dot(lhs[...], rhs[...], preferred_element_type=F32)
        high, low = split(wide[:32] + wide[32:])
        both = jnp.concatenate([high, low], axis=0)
        s_ref[:, pl.ds(pl.multiple_of(x * cells, cells), cells)] = both
        acc[...] += lax.dot_general(both, both, (((1,), (1,)), ((), ())), preferred_element_type=F32)

    total = acc[0:32, :] + acc[32:64, :]
    gram = total[:, :32] + total[:, 32:]
    g_ref[...] = jnp.concatenate([gram[8 * q:8 * q + 8, :] for q in range(4)], axis=1)


def reduce_kernel(sizes, g_ref, t_ref, one, two, send1, recv1, send2, recv2):
    n_s, n_y, n_z = sizes
    i_s, i_y, i_z = [lax.axis_index(name) for name in AXES]
    count = n_s * n_y
    me = i_s * n_y + i_y

    def plane_peer(k):
        other = lax.rem(me + k, count)
        return other, {"stream": other // n_y, "span": lax.rem(other, n_y)}

    def depth_peer(k):
        other = lax.rem(i_z + k, n_z)
        return other, {"depth": other}

    barrier = pltpu.get_barrier_semaphore()
    for k in range(1, count):
        pl.semaphore_signal(barrier, inc=1, device_id=plane_peer(k)[1], device_id_type=MESH)
    for k in range(1, n_z):
        pl.semaphore_signal(barrier, inc=1, device_id=depth_peer(k)[1], device_id_type=MESH)
    one[me] = g_ref[...]
    pl.semaphore_wait(barrier, count - 1 + n_z - 1)

    def exchange(buf, mine, number, peer_of, send, recv):
        copies = []
        for k in range(1, number):
            copy = pltpu.make_async_remote_copy(
                src_ref=buf.at[mine], dst_ref=buf.at[mine], send_sem=send.at[k], recv_sem=recv.at[k],
                device_id=peer_of(k)[1], device_id_type=MESH)
            copy.start()
            copies.append(copy)
        for copy in copies:
            copy.wait()
        total = buf[0]
        for k in range(1, number):
            total = total + buf[k]
        return total

    two[i_z] = exchange(one, me, count, plane_peer, send1, recv1)
    t_ref[...] = exchange(two, i_z, n_z, depth_peer, send2, recv2)


def factor(gram):
    lane = lax.broadcasted_iota(jnp.int32, (32, 128), 1)
    row = lax.broadcasted_iota(jnp.int32, (32, 128), 0)
    work = jnp.where(lane < 32, gram, jnp.where(lane - 32 == row, 1.0, 0.0))
    scale = jnp.zeros((32, 128), F32)
    for base in range(0, 32, 8):
        cols = [jnp.broadcast_to(work[:, base + q:base + q + 1], (32, 128)) for q in range(8)]
        for q in range(8):
            j = base + q
            pivot = jnp.broadcast_to(cols[q][j:j + 1, :], (32, 128))
            ratio = jnp.where(row > j, cols[q] * (1.0 / pivot), 0.0)
            for t in range(q + 1, 8):
                cols[t] = cols[t] - ratio * cols[t][j:j + 1, :]
            work = work - ratio * work[j:j + 1, :]
            scale = jnp.where(row == j, pivot, scale)
    return pltpu.roll(work, 96, 1) * lax.rsqrt(scale)


def basis_kernel(cells, planes, t_ref, s_ref, o_ref, stage, sems):
    packed = t_ref[...] * (1.0 / cells)
    gram = jnp.concatenate([packed if q == 0 else pltpu.roll(packed, 128 - 32 * q, 1) for q in range(4)], axis=0)
    inverse = factor(gram)[:, :32]
    high, low = split(inverse)
    left = jnp.concatenate(
        [jnp.concatenate([high, high], axis=1), jnp.concatenate([low, low], axis=1)], axis=0)
    rows = o_ref.shape[2]
    flat = stage.reshape(32 * planes * rows, 128)
    copies = []
    for x in range(planes):
        wide = jnp.dot(left, s_ref[:, x * rows * 128:(x + 1) * rows * 128], preferred_element_type=F32)
        block = wide[:32] + wide[32:]
        for y in range(rows):
            flat[pl.ds(x * rows + y, 32, stride=planes * rows), :] = block[:, 128 * y:128 * y + 128]
        copy = pltpu.make_async_copy(stage.at[:, pl.ds(x * rows, rows), :], o_ref.at[:, x], sems.at[x])
        copy.start()
        copies.append(copy)
    for copy in copies:
        copy.wait()


def body(sizes, forward, adjoint, weights):
    _, planes, rows, depth = forward.shape
    half = 3 * planes
    plane_count = sizes[0] * sizes[1]
    cells = planes * rows * depth * plane_count * sizes[2]
    hx, hy, hz = pl.pallas_call(
        functools.partial(halo_kernel, sizes),
        out_shape=(
            jax.ShapeDtypeStruct((2, 6, 2, rows, depth), F32),
            jax.ShapeDtypeStruct((2, 2, 2 * half, depth), F32),
            jax.ShapeDtypeStruct((2, 2, rows, depth), F32)),
        in_specs=[VMEM] * 2,
        out_specs=(VMEM,) * 3,
        scratch_shapes=[
            pltpu.VMEM((2, 2, 2 * half, depth), F32),
            pltpu.VMEM((2, 2, rows, depth), F32),
            pltpu.SemaphoreType.DMA((8,)),
            pltpu.SemaphoreType.DMA((8,))],
        compiler_params=pltpu.CompilerParams(collective_id=0, has_side_effects=True, vmem_limit_bytes=LIMIT),
        name="halo",
    )(forward, adjoint)
    snaps, gram = pl.pallas_call(
        snap_kernel,
        out_shape=(
            jax.ShapeDtypeStruct((64, planes * rows * depth), BF16),
            jax.ShapeDtypeStruct((8, 128), F32)),
        in_specs=[VMEM] * 6,
        out_specs=(VMEM,) * 2,
        scratch_shapes=[
            pltpu.VMEM((6, planes + 4, rows, depth), F32),
            pltpu.VMEM((2 * half, rows + 16, depth), F32),
            pltpu.VMEM((rows * 32, depth), F32),
            pltpu.VMEM((176, rows * depth), BF16),
            pltpu.VMEM((64, 176), BF16),
            pltpu.VMEM((64, 64), F32)],
        compiler_params=pltpu.CompilerParams(vmem_limit_bytes=LIMIT),
        name="snap",
    )(forward, adjoint, hx, hy, hz, weights)
    total = pl.pallas_call(
        functools.partial(reduce_kernel, sizes),
        out_shape=jax.ShapeDtypeStruct((8, 128), F32),
        in_specs=[VMEM],
        out_specs=VMEM,
        scratch_shapes=[
            pltpu.VMEM((plane_count, 8, 128), F32),
            pltpu.VMEM((sizes[2], 8, 128), F32),
            pltpu.SemaphoreType.DMA((plane_count,)),
            pltpu.SemaphoreType.DMA((plane_count,)),
            pltpu.SemaphoreType.DMA((sizes[2],)),
            pltpu.SemaphoreType.DMA((sizes[2],))],
        compiler_params=pltpu.CompilerParams(collective_id=1, has_side_effects=True, vmem_limit_bytes=LIMIT),
        name="reduce",
    )(gram)
    return pl.pallas_call(
        functools.partial(basis_kernel, cells, planes),
        out_shape=jax.ShapeDtypeStruct((32, planes, rows, depth), F32),
        in_specs=[VMEM] * 2,
        out_specs=pl.BlockSpec(memory_space=pl.ANY),
        scratch_shapes=[
            pltpu.VMEM((32, planes * rows, depth), F32),
            pltpu.SemaphoreType.DMA((planes,))],
        compiler_params=pltpu.CompilerParams(vmem_limit_bytes=LIMIT),
        name="basis",
    )(total, snaps)


def solution(mesh):
    sizes = tuple(mesh.shape[name] for name in AXES)
    in_specs = (P(None, *AXES), P(None, *AXES), P())
    return jax.shard_map(
        functools.partial(body, sizes), mesh=mesh, in_specs=in_specs, out_specs=P(None, *AXES), check_vma=False)
```

```python
import functools

import jax
import jax.numpy as jnp
from jax import lax
from jax.experimental import pallas as pl
from jax.experimental.pallas import tpu as pltpu
from jax.sharding import PartitionSpec as P

MESH = pl.DeviceIdType.MESH
F32 = jnp.float32
BF16 = jnp.bfloat16
AXES = ("stream", "span", "depth")
VMEM = pl.BlockSpec(memory_space=pltpu.VMEM)
LIMIT = 48 * 1024 * 1024


def split(value):
    high = value.astype(BF16)
    low = (value - high.astype(F32)).astype(BF16)
    return high, low


def snap_kernel(sizes, f_ref, a_ref, w_ref, s_ref, t_ref, px, py, hy, hz, ysend, zsend, wv, gs, rhs, lhs, acc,
                one, two, local, send, recv, send1, recv1, send2, recv2):
    n_s, n_y, n_z = sizes
    i_s, i_y, i_z = [lax.axis_index(name) for name in AXES]
    count = n_s * n_y
    me = i_s * n_y + i_y
    planes, rows = f_ref.shape[1], f_ref.shape[2]
    half = 3 * planes
    cells = rows * 128
    tall = rows + 16

    def plane_peer(k):
        other = lax.rem(me + k, count)
        return {"stream": other // n_y, "span": lax.rem(other, n_y)}

    def depth_peer(k):
        return {"depth": lax.rem(i_z + k, n_z)}

    barrier = pltpu.get_barrier_semaphore()
    for k in range(1, count):
        pl.semaphore_signal(barrier, inc=1, device_id=plane_peer(k), device_id_type=MESH)
    for k in range(1, n_z):
        pl.semaphore_signal(barrier, inc=1, device_id=depth_peer(k), device_id_type=MESH)

    loads = []

    def load(src, dst):
        copy = pltpu.make_async_copy(src, dst, local.at[len(loads)])
        copy.start()
        loads.append(copy)

    for k, ref in enumerate((f_ref, a_ref)):
        for c in range(3):
            m = 3 * k + c
            load(ref.at[c], py.at[m * planes:(m + 1) * planes, 8:8 + rows])
        load(ref, px.at[3 * k:3 * k + 3, 2:planes + 2])
    load(w_ref, wv)
    for copy in loads:
        copy.wait()

    flat = py.reshape(2 * half * tall, 128)
    for j in range(2):
        ysend[0, j] = flat[pl.ds(6 + rows + j, 2 * half, stride=tall), :]
        ysend[1, j] = flat[pl.ds(8 + j, 2 * half, stride=tall), :]
    lane = lax.broadcasted_iota(jnp.int32, (rows, 128), 1)
    for k in range(2):
        last = jnp.zeros((rows, 128), F32)
        first = jnp.zeros((rows, 128), F32)
        for i in range(half):
            own = py[k * half + i, 8:8 + rows, :]
            head = jnp.where(lane == 0, -own, 8.0 * pltpu.roll(own, 1, 1) - own)
            tail = jnp.where(lane == 126, own - 8.0 * pltpu.roll(own, 127, 1), own)
            head = pltpu.roll(head, 4 * i, 1) if i else head
            tail = pltpu.roll(tail, (4 * i + 4) % 128, 1)
            first = jnp.where(lane // 4 == i, head, first)
            last = jnp.where(lane // 4 == i, tail, last)
        zsend[0, k] = last
        zsend[1, k] = first

    pl.semaphore_wait(barrier, count - 1 + n_z - 1)
    copies = []

    def push(src, dst, peer):
        n = len(copies)
        copy = pltpu.make_async_remote_copy(
            src_ref=src, dst_ref=dst, send_sem=send.at[n], recv_sem=recv.at[n],
            device_id=peer, device_id_type=MESH)
        copy.start()
        copies.append(copy)

    def sides(name, size, mine):
        return {name: lax.rem(mine + 1, size)}, {name: lax.rem(mine + size - 1, size)}

    after_x, before_x = sides("stream", n_s, i_s)
    after_y, before_y = sides("span", n_y, i_y)
    after_z, before_z = sides("depth", n_z, i_z)
    push(ysend.at[0], hy.at[0], after_y)
    push(ysend.at[1], hy.at[1], before_y)
    push(zsend.at[0], hz.at[0], after_z)
    push(zsend.at[1], hz.at[1], before_z)
    for k, ref in enumerate((f_ref, a_ref)):
        push(ref.at[:, planes - 2:planes], px.at[3 * k:3 * k + 3, 0:2], after_x)
    for k, ref in enumerate((f_ref, a_ref)):
        push(ref.at[:, 0:2], px.at[3 * k:3 * k + 3, planes + 2:planes + 4], before_x)

    row = lax.broadcasted_iota(jnp.int32, (81, 176), 0)
    col = lax.broadcasted_iota(jnp.int32, (81, 176), 1)
    block, r = col // 16, col % 8
    source = jnp.where(block < 9, block * 9 + r, jnp.where(block == 9, r * 9 + 8, 80))
    keep = (row == source) & ((block < 10) | (r == 0))
    pick = jnp.where(keep, 1.0, 0.0).astype(BF16)
    w_high, w_low = split(wv[...] * (1.0 / 144.0))
    lhs[0:32, :] = jnp.dot(w_high, pick, preferred_element_type=F32).astype(BF16)
    lhs[32:64, :] = jnp.dot(w_low, pick, preferred_element_type=F32).astype(BF16)
    acc[...] = jnp.zeros_like(acc)

    for copy in copies[:4]:
        copy.wait()
    for j in range(2):
        flat[pl.ds(6 + j, 2 * half, stride=tall), :] = hy[0, j]
        flat[pl.ds(8 + rows + j, 2 * half, stride=tall), :] = hy[1, j]

    def stencil(m2, m1, p1, p2):
        return 8.0 * (p1 - m1) - (p2 - m2)

    def plane(x):
        for k in range(2):
            halo_z = jnp.where(lane % 4 < 2, hz[1, k], hz[0, k])
            for c in range(3):
                m = 3 * k + c
                own = px[m, x + 2]
                dx = stencil(px[m, x], px[m, x + 1], px[m, x + 3], px[m, x + 4])
                i = m * planes + x
                dy = stencil(*[py[i, 8 + o:8 + o + rows, :] for o in (-2, -1, 1, 2)])
                p1 = jnp.where(lane == 127, 0.0, pltpu.roll(own, 127, 1))
                p2 = jnp.where(lane >= 126, 0.0, pltpu.roll(own, 126, 1))
                m1 = jnp.where(lane == 0, 0.0, pltpu.roll(own, 1, 1))
                m2 = jnp.where(lane <= 1, 0.0, pltpu.roll(own, 2, 1))
                edge = pltpu.roll(halo_z, lax.rem(254 - 4 * (c * planes + x), 128), 1)
                dz = stencil(m2, m1, p1, p2) + jnp.where((lane < 2) | (lane >= 126), edge, 0.0)
                for d, slope in enumerate((dx, dy, dz)):
                    gs[pl.ds(16 * k + 3 * c + d, rows, stride=32), :] = slope
        for y in range(rows):
            base = 32 * y
            f8 = gs[base:base + 8, :]
            a8 = gs[base + 16:base + 24, :]
            a_end = gs[base + 24:base + 25, :]
            for n in range(11):
                if n < 9:
                    part = gs[base + n:base + n + 1, :] * a8
                elif n == 9:
                    part = f8 * a_end
                else:
                    part = jnp.broadcast_to(gs[base + 8:base + 9, :] * a_end, (8, 128))
                high = part.astype(BF16).astype(F32)
                both = jnp.concatenate([high, part - high], axis=0).astype(BF16)
                rhs[16 * n:16 * n + 16, 128 * y:128 * y + 128] = both
        wide = jnp.dot(lhs[...], rhs[...], preferred_element_type=F32)
        high, low = split(wide[:32] + wide[32:])
        both = jnp.concatenate([high, low], axis=0)
        s_ref[:, pl.ds(pl.multiple_of(x * cells, cells), cells)] = both
        acc[...] += lax.dot_general(both, both, (((1,), (1,)), ((), ())), preferred_element_type=F32)

    pl.loop(2, planes - 2)(plane)
    for copy in copies[4:6]:
        copy.wait()
    pl.loop(0, 2)(plane)
    for copy in copies[6:8]:
        copy.wait()
    pl.loop(planes - 2, planes)(plane)

    total = acc[0:32, :] + acc[32:64, :]
    gram = total[:, :32] + total[:, 32:]
    one[me] = jnp.concatenate([gram[8 * q:8 * q + 8, :] for q in range(4)], axis=1)

    def exchange(buf, mine, number, peer_of, send, recv):
        moves = []
        for k in range(1, number):
            copy = pltpu.make_async_remote_copy(
                src_ref=buf.at[mine], dst_ref=buf.at[mine], send_sem=send.at[k], recv_sem=recv.at[k],
                device_id=peer_of(k), device_id_type=MESH)
            copy.start()
            moves.append(copy)
        for copy in moves:
            copy.wait()
        total = buf[0]
        for k in range(1, number):
            total = total + buf[k]
        return total

    two[i_z] = exchange(one, me, count, plane_peer, send1, recv1)
    t_ref[...] = exchange(two, i_z, n_z, depth_peer, send2, recv2)


def factor(gram):
    lane = lax.broadcasted_iota(jnp.int32, (32, 128), 1)
    row = lax.broadcasted_iota(jnp.int32, (32, 128), 0)
    work = jnp.where(lane < 32, gram, jnp.where(lane - 32 == row, 1.0, 0.0))
    scale = jnp.zeros((32, 128), F32)
    for base in range(0, 32, 8):
        cols = [jnp.broadcast_to(work[:, base + q:base + q + 1], (32, 128)) for q in range(8)]
        for q in range(8):
            j = base + q
            pivot = jnp.broadcast_to(cols[q][j:j + 1, :], (32, 128))
            ratio = jnp.where(row > j, cols[q] * (1.0 / pivot), 0.0)
            for t in range(q + 1, 8):
                cols[t] = cols[t] - ratio * cols[t][j:j + 1, :]
            work = work - ratio * work[j:j + 1, :]
            scale = jnp.where(row == j, pivot, scale)
    return pltpu.roll(work, 96, 1) * lax.rsqrt(scale)


def basis_kernel(cells, planes, t_ref, s_ref, o_ref, stage, sems):
    packed = t_ref[...] * (1.0 / cells)
    gram = jnp.concatenate([packed if q == 0 else pltpu.roll(packed, 128 - 32 * q, 1) for q in range(4)], axis=0)
    inverse = factor(gram)[:, :32]
    high, low = split(inverse)
    left = jnp.concatenate(
        [jnp.concatenate([high, high], axis=1), jnp.concatenate([low, low], axis=1)], axis=0)
    rows = o_ref.shape[2]
    flat = stage.reshape(32 * planes * rows, 128)
    copies = []
    for x in range(planes):
        wide = jnp.dot(left, s_ref[:, x * rows * 128:(x + 1) * rows * 128], preferred_element_type=F32)
        block = wide[:32] + wide[32:]
        for y in range(rows):
            flat[pl.ds(x * rows + y, 32, stride=planes * rows), :] = block[:, 128 * y:128 * y + 128]
        copy = pltpu.make_async_copy(stage.at[:, pl.ds(x * rows, rows), :], o_ref.at[:, x], sems.at[x])
        copy.start()
        copies.append(copy)
    for copy in copies:
        copy.wait()


def body(sizes, forward, adjoint, weights):
    _, planes, rows, depth = forward.shape
    half = 3 * planes
    plane_count = sizes[0] * sizes[1]
    cells = planes * rows * depth * plane_count * sizes[2]
    total, snaps = pl.pallas_call(
        functools.partial(snap_kernel, sizes),
        out_shape=(
            jax.ShapeDtypeStruct((64, planes * rows * depth), BF16),
            jax.ShapeDtypeStruct((8, 128), F32)),
        in_specs=[pl.BlockSpec(memory_space=pltpu.HBM)] * 3,
        out_specs=(VMEM,) * 2,
        scratch_shapes=[
            pltpu.VMEM((6, planes + 4, rows, depth), F32),
            pltpu.VMEM((2 * half, rows + 16, depth), F32),
            pltpu.VMEM((2, 2, 2 * half, depth), F32),
            pltpu.VMEM((2, 2, rows, depth), F32),
            pltpu.VMEM((2, 2, 2 * half, depth), F32),
            pltpu.VMEM((2, 2, rows, depth), F32),
            pltpu.VMEM((32, 81), F32),
            pltpu.VMEM((rows * 32, depth), F32),
            pltpu.VMEM((176, rows * depth), BF16),
            pltpu.VMEM((64, 176), BF16),
            pltpu.VMEM((64, 64), F32),
            pltpu.VMEM((plane_count, 8, 128), F32),
            pltpu.VMEM((sizes[2], 8, 128), F32),
            pltpu.SemaphoreType.DMA((9,)),
            pltpu.SemaphoreType.DMA((8,)),
            pltpu.SemaphoreType.DMA((8,)),
            pltpu.SemaphoreType.DMA((plane_count,)),
            pltpu.SemaphoreType.DMA((plane_count,)),
            pltpu.SemaphoreType.DMA((sizes[2],)),
            pltpu.SemaphoreType.DMA((sizes[2],))],
        compiler_params=pltpu.CompilerParams(collective_id=0, has_side_effects=True, vmem_limit_bytes=LIMIT),
        name="snap",
    )(forward, adjoint, weights)[::-1]
    return pl.pallas_call(
        functools.partial(basis_kernel, cells, planes),
        out_shape=jax.ShapeDtypeStruct((32, planes, rows, depth), F32),
        in_specs=[VMEM] * 2,
        out_specs=pl.BlockSpec(memory_space=pl.ANY),
        scratch_shapes=[
            pltpu.VMEM((32, planes * rows, depth), F32),
            pltpu.SemaphoreType.DMA((planes,))],
        compiler_params=pltpu.CompilerParams(vmem_limit_bytes=LIMIT),
        name="basis",
    )(total, snaps)


def solution(mesh):
    sizes = tuple(mesh.shape[name] for name in AXES)
    in_specs = (P(None, *AXES), P(None, *AXES), P())
    return jax.shard_map(
        functools.partial(body, sizes), mesh=mesh, in_specs=in_specs, out_specs=P(None, *AXES), check_vma=False)
```

```python
import functools

import jax
import jax.numpy as jnp
from jax import lax
from jax.experimental import pallas as pl
from jax.experimental.pallas import tpu as pltpu
from jax.sharding import PartitionSpec as P

MESH = pl.DeviceIdType.MESH
F32 = jnp.float32
BF16 = jnp.bfloat16
AXES = ("stream", "span", "depth")
HBM = pl.BlockSpec(memory_space=pltpu.HBM)
VMEM = pl.BlockSpec(memory_space=pltpu.VMEM)
LIMIT = 56 * 1024 * 1024


def split(value):
    high = value.astype(BF16)
    low = (value - high.astype(F32)).astype(BF16)
    return high, low


def snap_kernel(sizes, f_ref, a_ref, w_ref, s_out, t_ref, s_ref, px, py, hy, hz, ysend, zsend, wv, gs, rhs, lhs, acc,
                one, two, local, store, send, recv, send1, recv1, send2, recv2):
    n_s, n_y, n_z = sizes
    i_s, i_y, i_z = [lax.axis_index(name) for name in AXES]
    count = n_s * n_y
    me = i_s * n_y + i_y
    planes, rows = f_ref.shape[1], f_ref.shape[2]
    half = 3 * planes
    cells = rows * 128
    tall = rows + 16

    def plane_peer(k):
        other = lax.rem(me + k, count)
        return {"stream": other // n_y, "span": lax.rem(other, n_y)}

    def depth_peer(k):
        return {"depth": lax.rem(i_z + k, n_z)}

    barrier = pltpu.get_barrier_semaphore()
    for k in range(1, count):
        pl.semaphore_signal(barrier, inc=1, device_id=plane_peer(k), device_id_type=MESH)
    for k in range(1, n_z):
        pl.semaphore_signal(barrier, inc=1, device_id=depth_peer(k), device_id_type=MESH)

    loads = []

    def load(src, dst):
        copy = pltpu.make_async_copy(src, dst, local.at[len(loads)])
        copy.start()
        loads.append(copy)

    for k, ref in enumerate((f_ref, a_ref)):
        for c in range(3):
            m = 3 * k + c
            load(ref.at[c], py.at[m * planes:(m + 1) * planes, 8:8 + rows])
        load(ref, px.at[3 * k:3 * k + 3, 2:planes + 2])
    load(w_ref, wv)
    pl.semaphore_wait(barrier, count - 1 + n_z - 1)
    copies = []

    def push(src, dst, peer):
        n = len(copies)
        copy = pltpu.make_async_remote_copy(
            src_ref=src, dst_ref=dst, send_sem=send.at[n], recv_sem=recv.at[n],
            device_id=peer, device_id_type=MESH)
        copy.start()
        copies.append(copy)

    def sides(name, size, mine):
        return {name: lax.rem(mine + 1, size)}, {name: lax.rem(mine + size - 1, size)}

    after_x, before_x = sides("stream", n_s, i_s)
    after_y, before_y = sides("span", n_y, i_y)
    after_z, before_z = sides("depth", n_z, i_z)
    for k, ref in enumerate((f_ref, a_ref)):
        push(ref.at[:, planes - 2:planes], px.at[3 * k:3 * k + 3, 0:2], after_x)
    for k, ref in enumerate((f_ref, a_ref)):
        push(ref.at[:, 0:2], px.at[3 * k:3 * k + 3, planes + 2:planes + 4], before_x)

    for copy in loads:
        copy.wait()
    flat = py.reshape(2 * half * tall, 128)
    for j in range(2):
        ysend[0, j] = flat[pl.ds(6 + rows + j, 2 * half, stride=tall), :]
        ysend[1, j] = flat[pl.ds(8 + j, 2 * half, stride=tall), :]
    lane = lax.broadcasted_iota(jnp.int32, (rows, 128), 1)
    for k in range(2):
        last = jnp.zeros((rows, 128), F32)
        first = jnp.zeros((rows, 128), F32)
        for i in range(half):
            own = py[k * half + i, 8:8 + rows, :]
            head = jnp.where(lane == 0, -own, 8.0 * pltpu.roll(own, 1, 1) - own)
            tail = jnp.where(lane == 126, own - 8.0 * pltpu.roll(own, 127, 1), own)
            head = pltpu.roll(head, 4 * i, 1) if i else head
            tail = pltpu.roll(tail, (4 * i + 4) % 128, 1)
            first = jnp.where(lane // 4 == i, head, first)
            last = jnp.where(lane // 4 == i, tail, last)
        zsend[0, k] = last
        zsend[1, k] = first

    push(ysend.at[0], hy.at[0], after_y)
    push(ysend.at[1], hy.at[1], before_y)
    push(zsend.at[0], hz.at[0], after_z)
    push(zsend.at[1], hz.at[1], before_z)

    row = lax.broadcasted_iota(jnp.int32, (81, 176), 0)
    col = lax.broadcasted_iota(jnp.int32, (81, 176), 1)
    block, r = col // 16, col % 8
    source = jnp.where(block < 9, block * 9 + r, jnp.where(block == 9, r * 9 + 8, 80))
    keep = (row == source) & ((block < 10) | (r == 0))
    pick = jnp.where(keep, 1.0, 0.0).astype(BF16)
    w_high, w_low = split(wv[...] * (1.0 / 144.0))
    lhs[0:32, :] = jnp.dot(w_high, pick, preferred_element_type=F32).astype(BF16)
    lhs[32:64, :] = jnp.dot(w_low, pick, preferred_element_type=F32).astype(BF16)
    acc[...] = jnp.zeros_like(acc)

    for copy in copies[4:8]:
        copy.wait()
    for j in range(2):
        flat[pl.ds(6 + j, 2 * half, stride=tall), :] = hy[0, j]
        flat[pl.ds(8 + rows + j, 2 * half, stride=tall), :] = hy[1, j]

    def stencil(m2, m1, p1, p2):
        return 8.0 * (p1 - m1) - (p2 - m2)

    def plane(x):
        for k in range(2):
            halo_z = jnp.where(lane % 4 < 2, hz[1, k], hz[0, k])
            for c in range(3):
                m = 3 * k + c
                own = px[m, x + 2]
                dx = stencil(px[m, x], px[m, x + 1], px[m, x + 3], px[m, x + 4])
                i = m * planes + x
                dy = stencil(*[py[i, 8 + o:8 + o + rows, :] for o in (-2, -1, 1, 2)])
                p1 = jnp.where(lane == 127, 0.0, pltpu.roll(own, 127, 1))
                p2 = jnp.where(lane >= 126, 0.0, pltpu.roll(own, 126, 1))
                m1 = jnp.where(lane == 0, 0.0, pltpu.roll(own, 1, 1))
                m2 = jnp.where(lane <= 1, 0.0, pltpu.roll(own, 2, 1))
                edge = pltpu.roll(halo_z, lax.rem(254 - 4 * (c * planes + x), 128), 1)
                dz = stencil(m2, m1, p1, p2) + jnp.where((lane < 2) | (lane >= 126), edge, 0.0)
                for d, slope in enumerate((dx, dy, dz)):
                    gs[pl.ds(16 * k + 3 * c + d, rows, stride=32), :] = slope
        for y in range(rows):
            base = 32 * y
            f8 = gs[base:base + 8, :]
            a8 = gs[base + 16:base + 24, :]
            a_end = gs[base + 24:base + 25, :]
            for n in range(11):
                if n < 9:
                    part = gs[base + n:base + n + 1, :] * a8
                elif n == 9:
                    part = f8 * a_end
                else:
                    part = jnp.broadcast_to(gs[base + 8:base + 9, :] * a_end, (8, 128))
                high = part.astype(BF16).astype(F32)
                both = jnp.concatenate([high, part - high], axis=0).astype(BF16)
                rhs[16 * n:16 * n + 16, 128 * y:128 * y + 128] = both
        wide = jnp.dot(lhs[...], rhs[...], preferred_element_type=F32)
        high, low = split(wide[:32] + wide[32:])
        both = jnp.concatenate([high, low], axis=0)
        s_ref[:, pl.ds(pl.multiple_of(x * cells, cells), cells)] = both
        acc[...] += lax.dot_general(both, both, (((1,), (1,)), ((), ())), preferred_element_type=F32)

    def keep_plane(x):
        part = pl.ds(x * cells, cells)
        return pltpu.make_async_copy(s_ref.at[:, part], s_out.at[:, part], store.at[x])

    pl.loop(2, planes - 2)(plane)
    for x in range(2, planes - 2):
        keep_plane(x).start()
    for copy in copies[0:2]:
        copy.wait()
    pl.loop(0, 2)(plane)
    for x in range(2):
        keep_plane(x).start()
    for copy in copies[2:4]:
        copy.wait()
    pl.loop(planes - 2, planes)(plane)
    for x in range(planes - 2, planes):
        keep_plane(x).start()

    total = acc[0:32, :] + acc[32:64, :]
    gram = total[:, :32] + total[:, 32:]
    one[me] = jnp.concatenate([gram[8 * q:8 * q + 8, :] for q in range(4)], axis=1)

    def exchange(buf, mine, number, peer_of, send, recv):
        moves = []
        for k in range(1, number):
            copy = pltpu.make_async_remote_copy(
                src_ref=buf.at[mine], dst_ref=buf.at[mine], send_sem=send.at[k], recv_sem=recv.at[k],
                device_id=peer_of(k), device_id_type=MESH)
            copy.start()
            moves.append(copy)
        for copy in moves:
            copy.wait()
        total = buf[0]
        for k in range(1, number):
            total = total + buf[k]
        return total

    two[i_z] = exchange(one, me, count, plane_peer, send1, recv1)
    t_ref[...] = exchange(two, i_z, n_z, depth_peer, send2, recv2)
    for x in range(planes):
        keep_plane(x).wait()


def factor(gram):
    lane = lax.broadcasted_iota(jnp.int32, (32, 128), 1)
    row = lax.broadcasted_iota(jnp.int32, (32, 128), 0)
    work = jnp.where(lane < 32, gram, jnp.where(lane - 32 == row, 1.0, 0.0))
    scale = jnp.zeros((32, 128), F32)
    for base in range(0, 32, 8):
        cols = [jnp.broadcast_to(work[:, base + q:base + q + 1], (32, 128)) for q in range(8)]
        for q in range(8):
            j = base + q
            pivot = jnp.broadcast_to(cols[q][j:j + 1, :], (32, 128))
            ratio = jnp.where(row > j, cols[q] * (1.0 / pivot), 0.0)
            for t in range(q + 1, 8):
                cols[t] = cols[t] - ratio * cols[t][j:j + 1, :]
            work = work - ratio * work[j:j + 1, :]
            scale = jnp.where(row == j, pivot, scale)
    return pltpu.roll(work, 96, 1) * lax.rsqrt(scale)


def basis_kernel(cells, planes, t_ref, s_in, o_ref, s_ref, stage, loads, sems):
    width = s_in.shape[1] // planes

    def fetch(x):
        part = pl.ds(x * width, width)
        return pltpu.make_async_copy(s_in.at[:, part], s_ref.at[:, part], loads.at[x])

    for x in range(planes):
        fetch(x).start()
    packed = t_ref[...] * (1.0 / cells)
    gram = jnp.concatenate([packed if q == 0 else pltpu.roll(packed, 128 - 32 * q, 1) for q in range(4)], axis=0)
    inverse = factor(gram)[:, :32]
    high, low = split(inverse)
    left = jnp.concatenate(
        [jnp.concatenate([high, high], axis=1), jnp.concatenate([low, low], axis=1)], axis=0)
    rows = o_ref.shape[2]
    flat = stage.reshape(32 * planes * rows, 128)
    copies = []
    for x in range(planes):
        fetch(x).wait()
        wide = jnp.dot(left, s_ref[:, x * width:(x + 1) * width], preferred_element_type=F32)
        block = wide[:32] + wide[32:]
        for y in range(rows):
            flat[pl.ds(x * rows + y, 32, stride=planes * rows), :] = block[:, 128 * y:128 * y + 128]
        copy = pltpu.make_async_copy(stage.at[:, pl.ds(x * rows, rows), :], o_ref.at[:, x], sems.at[x])
        copy.start()
        copies.append(copy)
    for copy in copies:
        copy.wait()


def body(sizes, forward, adjoint, weights):
    _, planes, rows, depth = forward.shape
    half = 3 * planes
    plane_count = sizes[0] * sizes[1]
    cells = planes * rows * depth * plane_count * sizes[2]
    total, snaps = pl.pallas_call(
        functools.partial(snap_kernel, sizes),
        out_shape=(
            jax.ShapeDtypeStruct((64, planes * rows * depth), BF16),
            jax.ShapeDtypeStruct((8, 128), F32)),
        in_specs=[HBM] * 3,
        out_specs=(HBM, VMEM),
        scratch_shapes=[
            pltpu.VMEM((64, planes * rows * depth), BF16),
            pltpu.VMEM((6, planes + 4, rows, depth), F32),
            pltpu.VMEM((2 * half, rows + 16, depth), F32),
            pltpu.VMEM((2, 2, 2 * half, depth), F32),
            pltpu.VMEM((2, 2, rows, depth), F32),
            pltpu.VMEM((2, 2, 2 * half, depth), F32),
            pltpu.VMEM((2, 2, rows, depth), F32),
            pltpu.VMEM((32, 81), F32),
            pltpu.VMEM((rows * 32, depth), F32),
            pltpu.VMEM((176, rows * depth), BF16),
            pltpu.VMEM((64, 176), BF16),
            pltpu.VMEM((64, 64), F32),
            pltpu.VMEM((plane_count, 8, 128), F32),
            pltpu.VMEM((sizes[2], 8, 128), F32),
            pltpu.SemaphoreType.DMA((9,)),
            pltpu.SemaphoreType.DMA((planes,)),
            pltpu.SemaphoreType.DMA((8,)),
            pltpu.SemaphoreType.DMA((8,)),
            pltpu.SemaphoreType.DMA((plane_count,)),
            pltpu.SemaphoreType.DMA((plane_count,)),
            pltpu.SemaphoreType.DMA((sizes[2],)),
            pltpu.SemaphoreType.DMA((sizes[2],))],
        compiler_params=pltpu.CompilerParams(collective_id=0, has_side_effects=True, vmem_limit_bytes=LIMIT),
        name="snap",
    )(forward, adjoint, weights)[::-1]
    return pl.pallas_call(
        functools.partial(basis_kernel, cells, planes),
        out_shape=jax.ShapeDtypeStruct((32, planes, rows, depth), F32),
        in_specs=[VMEM, HBM],
        out_specs=HBM,
        scratch_shapes=[
            pltpu.VMEM((64, planes * rows * depth), BF16),
            pltpu.VMEM((32, planes * rows, depth), F32),
            pltpu.SemaphoreType.DMA((planes,)),
            pltpu.SemaphoreType.DMA((planes,))],
        compiler_params=pltpu.CompilerParams(vmem_limit_bytes=LIMIT),
        name="basis",
    )(total, snaps)


def solution(mesh):
    sizes = tuple(mesh.shape[name] for name in AXES)
    in_specs = (P(None, *AXES), P(None, *AXES), P())
    return jax.shard_map(
        functools.partial(body, sizes), mesh=mesh, in_specs=in_specs, out_specs=P(None, *AXES), check_vma=False)
```

```python
import functools

import jax
import jax.numpy as jnp
from jax import lax
from jax.experimental import pallas as pl
from jax.experimental.pallas import tpu as pltpu
from jax.sharding import PartitionSpec as P

MESH = pl.DeviceIdType.MESH
F32 = jnp.float32
BF16 = jnp.bfloat16
AXES = ("stream", "span", "depth")
HBM = pl.BlockSpec(memory_space=pltpu.HBM)
VMEM = pl.BlockSpec(memory_space=pltpu.VMEM)
LIMIT = 48 * 1024 * 1024


def split(value):
    high = value.astype(BF16)
    low = (value - high.astype(F32)).astype(BF16)
    return high, low


def snap_kernel(sizes, f_ref, a_ref, w_ref, s_ref, t_ref, px, py, hy, hz, ysend, zsend, wv, gs, rhs, lhs, acc,
                one, two, local, send, recv, send1, recv1, send2, recv2):
    n_s, n_y, n_z = sizes
    i_s, i_y, i_z = [lax.axis_index(name) for name in AXES]
    count = n_s * n_y
    me = i_s * n_y + i_y
    planes, rows = f_ref.shape[1], f_ref.shape[2]
    half = 3 * planes
    cells = rows * 128
    tall = rows + 16

    def plane_peer(k):
        other = lax.rem(me + k, count)
        return {"stream": other // n_y, "span": lax.rem(other, n_y)}

    def depth_peer(k):
        return {"depth": lax.rem(i_z + k, n_z)}

    barrier = pltpu.get_barrier_semaphore()
    for k in range(1, count):
        pl.semaphore_signal(barrier, inc=1, device_id=plane_peer(k), device_id_type=MESH)
    for k in range(1, n_z):
        pl.semaphore_signal(barrier, inc=1, device_id=depth_peer(k), device_id_type=MESH)

    loads = []

    def load(src, dst):
        copy = pltpu.make_async_copy(src, dst, local.at[len(loads)])
        copy.start()
        loads.append(copy)

    for k, ref in enumerate((f_ref, a_ref)):
        for c in range(3):
            m = 3 * k + c
            load(ref.at[c], py.at[m * planes:(m + 1) * planes, 8:8 + rows])
        load(ref, px.at[3 * k:3 * k + 3, 2:planes + 2])
    load(w_ref, wv)
    pl.semaphore_wait(barrier, count - 1 + n_z - 1)
    copies = []

    def push(src, dst, peer):
        n = len(copies)
        copy = pltpu.make_async_remote_copy(
            src_ref=src, dst_ref=dst, send_sem=send.at[n], recv_sem=recv.at[n],
            device_id=peer, device_id_type=MESH)
        copy.start()
        copies.append(copy)

    def sides(name, size, mine):
        return {name: lax.rem(mine + 1, size)}, {name: lax.rem(mine + size - 1, size)}

    after_x, before_x = sides("stream", n_s, i_s)
    after_y, before_y = sides("span", n_y, i_y)
    after_z, before_z = sides("depth", n_z, i_z)
    for k, ref in enumerate((f_ref, a_ref)):
        push(ref.at[:, planes - 2:planes], px.at[3 * k:3 * k + 3, 0:2], after_x)
    for k, ref in enumerate((f_ref, a_ref)):
        push(ref.at[:, 0:2], px.at[3 * k:3 * k + 3, planes + 2:planes + 4], before_x)

    for copy in loads:
        copy.wait()
    flat = py.reshape(2 * half * tall, 128)
    for j in range(2):
        ysend[0, j] = flat[pl.ds(6 + rows + j, 2 * half, stride=tall), :]
        ysend[1, j] = flat[pl.ds(8 + j, 2 * half, stride=tall), :]
    lane = lax.broadcasted_iota(jnp.int32, (rows, 128), 1)
    for k in range(2):
        last = jnp.zeros((rows, 128), F32)
        first = jnp.zeros((rows, 128), F32)
        for i in range(half):
            own = py[k * half + i, 8:8 + rows, :]
            head = jnp.where(lane == 0, -own, 8.0 * pltpu.roll(own, 1, 1) - own)
            tail = jnp.where(lane == 126, own - 8.0 * pltpu.roll(own, 127, 1), own)
            head = pltpu.roll(head, 4 * i, 1) if i else head
            tail = pltpu.roll(tail, (4 * i + 4) % 128, 1)
            first = jnp.where(lane // 4 == i, head, first)
            last = jnp.where(lane // 4 == i, tail, last)
        zsend[0, k] = last
        zsend[1, k] = first

    push(ysend.at[0], hy.at[0], after_y)
    push(ysend.at[1], hy.at[1], before_y)
    push(zsend.at[0], hz.at[0], after_z)
    push(zsend.at[1], hz.at[1], before_z)

    row = lax.broadcasted_iota(jnp.int32, (81, 176), 0)
    col = lax.broadcasted_iota(jnp.int32, (81, 176), 1)
    block, r = col // 16, col % 8
    source = jnp.where(block < 9, block * 9 + r, jnp.where(block == 9, r * 9 + 8, 80))
    keep = (row == source) & ((block < 10) | (r == 0))
    pick = jnp.where(keep, 1.0, 0.0).astype(BF16)
    w_high, w_low = split(wv[...] * (1.0 / 144.0))
    lhs[0:32, :] = jnp.dot(w_high, pick, preferred_element_type=F32).astype(BF16)
    lhs[32:64, :] = jnp.dot(w_low, pick, preferred_element_type=F32).astype(BF16)
    acc[...] = jnp.zeros_like(acc)

    for copy in copies[4:8]:
        copy.wait()
    for j in range(2):
        flat[pl.ds(6 + j, 2 * half, stride=tall), :] = hy[0, j]
        flat[pl.ds(8 + rows + j, 2 * half, stride=tall), :] = hy[1, j]

    def stencil(m2, m1, p1, p2):
        return 8.0 * (p1 - m1) - (p2 - m2)

    def plane(x):
        for k in range(2):
            halo_z = jnp.where(lane % 4 < 2, hz[1, k], hz[0, k])
            for c in range(3):
                m = 3 * k + c
                own = px[m, x + 2]
                dx = stencil(px[m, x], px[m, x + 1], px[m, x + 3], px[m, x + 4])
                i = m * planes + x
                dy = stencil(*[py[i, 8 + o:8 + o + rows, :] for o in (-2, -1, 1, 2)])
                p1 = jnp.where(lane == 127, 0.0, pltpu.roll(own, 127, 1))
                p2 = jnp.where(lane >= 126, 0.0, pltpu.roll(own, 126, 1))
                m1 = jnp.where(lane == 0, 0.0, pltpu.roll(own, 1, 1))
                m2 = jnp.where(lane <= 1, 0.0, pltpu.roll(own, 2, 1))
                edge = pltpu.roll(halo_z, lax.rem(254 - 4 * (c * planes + x), 128), 1)
                dz = stencil(m2, m1, p1, p2) + jnp.where((lane < 2) | (lane >= 126), edge, 0.0)
                for d, slope in enumerate((dx, dy, dz)):
                    gs[pl.ds(16 * k + 3 * c + d, rows, stride=32), :] = slope
        for y in range(rows):
            base = 32 * y
            f8 = gs[base:base + 8, :]
            a8 = gs[base + 16:base + 24, :]
            a_end = gs[base + 24:base + 25, :]
            for n in range(11):
                if n < 9:
                    part = gs[base + n:base + n + 1, :] * a8
                elif n == 9:
                    part = f8 * a_end
                else:
                    part = jnp.broadcast_to(gs[base + 8:base + 9, :] * a_end, (8, 128))
                high = part.astype(BF16).astype(F32)
                both = jnp.concatenate([high, part - high], axis=0).astype(BF16)
                rhs[16 * n:16 * n + 16, 128 * y:128 * y + 128] = both
        wide = jnp.dot(lhs[...], rhs[...], preferred_element_type=F32)
        high, low = split(wide[:32] + wide[32:])
        both = jnp.concatenate([high, low], axis=0)
        s_ref[:, pl.ds(pl.multiple_of(x * cells, cells), cells)] = both
        acc[...] += lax.dot_general(both, both, (((1,), (1,)), ((), ())), preferred_element_type=F32)

    pl.loop(2, planes - 2)(plane)
    for copy in copies[0:2]:
        copy.wait()
    pl.loop(0, 2)(plane)
    for copy in copies[2:4]:
        copy.wait()
    pl.loop(planes - 2, planes)(plane)

    total = acc[0:32, :] + acc[32:64, :]
    gram = total[:, :32] + total[:, 32:]
    one[me] = jnp.concatenate([gram[8 * q:8 * q + 8, :] for q in range(4)], axis=1)

    def exchange(buf, mine, number, peer_of, send, recv):
        moves = []
        for k in range(1, number):
            copy = pltpu.make_async_remote_copy(
                src_ref=buf.at[mine], dst_ref=buf.at[mine], send_sem=send.at[k], recv_sem=recv.at[k],
                device_id=peer_of(k), device_id_type=MESH)
            copy.start()
            moves.append(copy)
        for copy in moves:
            copy.wait()
        total = buf[0]
        for k in range(1, number):
            total = total + buf[k]
        return total

    two[i_z] = exchange(one, me, count, plane_peer, send1, recv1)
    t_ref[...] = exchange(two, i_z, n_z, depth_peer, send2, recv2)


def factor(gram):
    lane = lax.broadcasted_iota(jnp.int32, (32, 128), 1)
    row = lax.broadcasted_iota(jnp.int32, (32, 128), 0)
    work = jnp.where(lane < 32, gram, jnp.where(lane - 32 == row, 1.0, 0.0))
    scale = jnp.zeros((32, 128), F32)
    for base in range(0, 32, 8):
        cols = [jnp.broadcast_to(work[:, base + q:base + q + 1], (32, 128)) for q in range(8)]
        for q in range(8):
            j = base + q
            pivot = jnp.broadcast_to(cols[q][j:j + 1, :], (32, 128))
            ratio = jnp.where(row > j, cols[q] * (1.0 / pivot), 0.0)
            for t in range(q + 1, 8):
                cols[t] = cols[t] - ratio * cols[t][j:j + 1, :]
            work = work - ratio * work[j:j + 1, :]
            scale = jnp.where(row == j, pivot, scale)
    return pltpu.roll(work, 96, 1) * lax.rsqrt(scale)


def basis_kernel(cells, planes, t_ref, s_ref, o_ref, stage, sems):
    width = s_ref.shape[1] // planes
    packed = t_ref[...] * (1.0 / cells)
    gram = jnp.concatenate([packed if q == 0 else pltpu.roll(packed, 128 - 32 * q, 1) for q in range(4)], axis=0)
    inverse = factor(gram)[:, :32]
    high, low = split(inverse)
    left = jnp.concatenate(
        [jnp.concatenate([high, high], axis=1), jnp.concatenate([low, low], axis=1)], axis=0)
    rows = o_ref.shape[2]
    flat = stage.reshape(32 * planes * rows, 128)
    copies = []
    for x in range(planes):
        wide = jnp.dot(left, s_ref[:, x * width:(x + 1) * width], preferred_element_type=F32)
        block = wide[:32] + wide[32:]
        for y in range(rows):
            flat[pl.ds(x * rows + y, 32, stride=planes * rows), :] = block[:, 128 * y:128 * y + 128]
        copy = pltpu.make_async_copy(stage.at[:, pl.ds(x * rows, rows), :], o_ref.at[:, x], sems.at[x])
        copy.start()
        copies.append(copy)
    for copy in copies:
        copy.wait()


def body(sizes, forward, adjoint, weights):
    _, planes, rows, depth = forward.shape
    half = 3 * planes
    plane_count = sizes[0] * sizes[1]
    cells = planes * rows * depth * plane_count * sizes[2]
    total, snaps = pl.pallas_call(
        functools.partial(snap_kernel, sizes),
        out_shape=(
            jax.ShapeDtypeStruct((64, planes * rows * depth), BF16),
            jax.ShapeDtypeStruct((8, 128), F32)),
        in_specs=[HBM] * 3,
        out_specs=(VMEM, VMEM),
        scratch_shapes=[
            pltpu.VMEM((6, planes + 4, rows, depth), F32),
            pltpu.VMEM((2 * half, rows + 16, depth), F32),
            pltpu.VMEM((2, 2, 2 * half, depth), F32),
            pltpu.VMEM((2, 2, rows, depth), F32),
            pltpu.VMEM((2, 2, 2 * half, depth), F32),
            pltpu.VMEM((2, 2, rows, depth), F32),
            pltpu.VMEM((32, 81), F32),
            pltpu.VMEM((rows * 32, depth), F32),
            pltpu.VMEM((176, rows * depth), BF16),
            pltpu.VMEM((64, 176), BF16),
            pltpu.VMEM((64, 64), F32),
            pltpu.VMEM((plane_count, 8, 128), F32),
            pltpu.VMEM((sizes[2], 8, 128), F32),
            pltpu.SemaphoreType.DMA((9,)),
            pltpu.SemaphoreType.DMA((8,)),
            pltpu.SemaphoreType.DMA((8,)),
            pltpu.SemaphoreType.DMA((plane_count,)),
            pltpu.SemaphoreType.DMA((plane_count,)),
            pltpu.SemaphoreType.DMA((sizes[2],)),
            pltpu.SemaphoreType.DMA((sizes[2],))],
        compiler_params=pltpu.CompilerParams(collective_id=0, has_side_effects=True, vmem_limit_bytes=LIMIT),
        name="snap",
    )(*[pltpu.with_memory_space_constraint(value, pltpu.HBM) for value in (forward, adjoint, weights)])[::-1]
    return pl.pallas_call(
        functools.partial(basis_kernel, cells, planes),
        out_shape=jax.ShapeDtypeStruct((32, planes, rows, depth), F32),
        in_specs=[VMEM, VMEM],
        out_specs=HBM,
        scratch_shapes=[
            pltpu.VMEM((32, planes * rows, depth), F32),
            pltpu.SemaphoreType.DMA((planes,))],
        compiler_params=pltpu.CompilerParams(vmem_limit_bytes=LIMIT),
        name="basis",
    )(total, snaps)


def solution(mesh):
    sizes = tuple(mesh.shape[name] for name in AXES)
    in_specs = (P(None, *AXES), P(None, *AXES), P())
    return jax.shard_map(
        functools.partial(body, sizes), mesh=mesh, in_specs=in_specs, out_specs=P(None, *AXES), check_vma=False)
```

```python
import functools

import jax
import jax.numpy as jnp
from jax import lax
from jax.experimental import pallas as pl
from jax.experimental.pallas import tpu as pltpu
from jax.sharding import PartitionSpec as P

MESH = pl.DeviceIdType.MESH
F32 = jnp.float32
BF16 = jnp.bfloat16
AXES = ("stream", "span", "depth")
HBM = pl.BlockSpec(memory_space=pltpu.HBM)
VMEM = pl.BlockSpec(memory_space=pltpu.VMEM)
LIMIT = 48 * 1024 * 1024


def split(value):
    high = value.astype(BF16)
    low = (value - high.astype(F32)).astype(BF16)
    return high, low


def snap_kernel(sizes, f_ref, a_ref, w_ref, s_ref, t_ref, px, py, hy, hz, ysend, zsend, wv, gs, sx, sz, lhs, acc,
                one, two, local, send, recv, send1, recv1, send2, recv2):
    n_s, n_y, n_z = sizes
    i_s, i_y, i_z = [lax.axis_index(name) for name in AXES]
    count = n_s * n_y
    me = i_s * n_y + i_y
    planes, rows = f_ref.shape[1], f_ref.shape[2]
    half = 3 * planes
    cells = rows * 128
    tall = rows + 16

    def plane_peer(k):
        other = lax.rem(me + k, count)
        return {"stream": other // n_y, "span": lax.rem(other, n_y)}

    def depth_peer(k):
        return {"depth": lax.rem(i_z + k, n_z)}

    barrier = pltpu.get_barrier_semaphore()
    for k in range(1, count):
        pl.semaphore_signal(barrier, inc=1, device_id=plane_peer(k), device_id_type=MESH)
    for k in range(1, n_z):
        pl.semaphore_signal(barrier, inc=1, device_id=depth_peer(k), device_id_type=MESH)

    loads = []

    def load(src, dst):
        copy = pltpu.make_async_copy(src, dst, local.at[len(loads)])
        copy.start()
        loads.append(copy)

    for k, ref in enumerate((f_ref, a_ref)):
        for c in range(3):
            m = 3 * k + c
            load(ref.at[c], py.at[m * planes:(m + 1) * planes, 8:8 + rows])
        load(ref, px.at[3 * k:3 * k + 3, 2:planes + 2])
    load(w_ref, wv)
    pl.semaphore_wait(barrier, count - 1 + n_z - 1)
    copies = []

    def push(src, dst, peer):
        n = len(copies)
        copy = pltpu.make_async_remote_copy(
            src_ref=src, dst_ref=dst, send_sem=send.at[n], recv_sem=recv.at[n],
            device_id=peer, device_id_type=MESH)
        copy.start()
        copies.append(copy)

    def sides(name, size, mine):
        return {name: lax.rem(mine + 1, size)}, {name: lax.rem(mine + size - 1, size)}

    after_x, before_x = sides("stream", n_s, i_s)
    after_y, before_y = sides("span", n_y, i_y)
    after_z, before_z = sides("depth", n_z, i_z)
    for k, ref in enumerate((f_ref, a_ref)):
        push(ref.at[:, planes - 2:planes], px.at[3 * k:3 * k + 3, 0:2], after_x)
    for k, ref in enumerate((f_ref, a_ref)):
        push(ref.at[:, 0:2], px.at[3 * k:3 * k + 3, planes + 2:planes + 4], before_x)

    for copy in loads:
        copy.wait()
    flat = py.reshape(2 * half * tall, 128)
    for j in range(2):
        ysend[0, j] = flat[pl.ds(6 + rows + j, 2 * half, stride=tall), :]
        ysend[1, j] = flat[pl.ds(8 + j, 2 * half, stride=tall), :]
    lane = lax.broadcasted_iota(jnp.int32, (rows, 128), 1)
    for k in range(2):
        last = jnp.zeros((rows, 128), F32)
        first = jnp.zeros((rows, 128), F32)
        for i in range(half):
            own = py[k * half + i, 8:8 + rows, :]
            head = jnp.where(lane == 0, -own, 8.0 * pltpu.roll(own, 1, 1) - own)
            tail = jnp.where(lane == 126, own - 8.0 * pltpu.roll(own, 127, 1), own)
            head = pltpu.roll(head, 4 * i, 1) if i else head
            tail = pltpu.roll(tail, (4 * i + 4) % 128, 1)
            first = jnp.where(lane // 4 == i, head, first)
            last = jnp.where(lane // 4 == i, tail, last)
        zsend[0, k] = last
        zsend[1, k] = first

    push(ysend.at[0], hy.at[0], after_y)
    push(ysend.at[1], hy.at[1], before_y)
    push(zsend.at[0], hz.at[0], after_z)
    push(zsend.at[1], hz.at[1], before_z)

    row = lax.broadcasted_iota(jnp.int32, (81, 176), 0)
    col = lax.broadcasted_iota(jnp.int32, (81, 176), 1)
    block, r = col // 16, col % 8
    source = jnp.where(block < 9, block * 9 + r, jnp.where(block == 9, r * 9 + 8, 80))
    keep = (row == source) & ((block < 10) | (r == 0))
    pick = jnp.where(keep, 1.0, 0.0).astype(BF16)
    w_high, w_low = split(wv[...] * (1.0 / 144.0))
    lhs[0:32, :] = jnp.dot(w_high, pick, preferred_element_type=F32).astype(BF16)
    lhs[32:64, :] = jnp.dot(w_low, pick, preferred_element_type=F32).astype(BF16)
    acc[...] = jnp.zeros_like(acc)

    def stencil(m2, m1, p1, p2):
        return 8.0 * (p1 - m1) - (p2 - m2)

    @pl.loop(0, planes)
    def _(x):
        for m in range(6):
            own = px[m, x + 2]
            p1 = jnp.where(lane == 127, 0.0, pltpu.roll(own, 127, 1))
            p2 = jnp.where(lane >= 126, 0.0, pltpu.roll(own, 126, 1))
            m1 = jnp.where(lane == 0, 0.0, pltpu.roll(own, 1, 1))
            m2 = jnp.where(lane <= 1, 0.0, pltpu.roll(own, 2, 1))
            sz[m * planes + x] = stencil(m2, m1, p1, p2)

    @pl.loop(2, planes - 2)
    def _(x):
        for m in range(6):
            sx[m * planes + x] = stencil(px[m, x], px[m, x + 1], px[m, x + 3], px[m, x + 4])

    for copy in copies[4:8]:
        copy.wait()
    for j in range(2):
        flat[pl.ds(6 + j, 2 * half, stride=tall), :] = hy[0, j]
        flat[pl.ds(8 + rows + j, 2 * half, stride=tall), :] = hy[1, j]

    def inner_x(x, k, c):
        m = 3 * k + c
        return stencil(px[m, x], px[m, x + 1], px[m, x + 3], px[m, x + 4])

    def plane(x, slot, ready):
        for k in range(2):
            halo_z = jnp.where(lane % 4 < 2, hz[1, k], hz[0, k])
            for c in range(3):
                i = (3 * k + c) * planes + x
                dx = sx[i] if ready else inner_x(x, k, c)
                dy = stencil(*[py[i, 8 + o:8 + o + rows, :] for o in (-2, -1, 1, 2)])
                edge = pltpu.roll(halo_z, lax.rem(254 - 4 * (c * planes + x), 128), 1)
                dz = sz[i] + jnp.where((lane < 2) | (lane >= 126), edge, 0.0)
                for d, slope in enumerate((dx, dy, dz)):
                    gs[slot, pl.ds(16 * k + 3 * c + d, rows, stride=32), :] = slope
        parts = []
        for pair in range(0, rows, 2):
            tiles = []
            for y in (pair, pair + 1):
                base = 32 * y
                f8 = gs[slot, base:base + 8, :]
                a8 = gs[slot, base + 16:base + 24, :]
                a_end = gs[slot, base + 24:base + 25, :]
                blocks = []
                for n in range(11):
                    if n < 9:
                        part = gs[slot, base + n:base + n + 1, :] * a8
                    elif n == 9:
                        part = f8 * a_end
                    else:
                        part = jnp.broadcast_to(gs[slot, base + 8:base + 9, :] * a_end, (8, 128))
                    high = part.astype(BF16).astype(F32)
                    blocks.append(jnp.concatenate([high, part - high], axis=0).astype(BF16))
                tiles.append(jnp.concatenate(blocks, axis=0))
            wide = jnp.dot(lhs[...], jnp.concatenate(tiles, axis=1), preferred_element_type=F32)
            high, low = split(wide[:32] + wide[32:])
            both = jnp.concatenate([high, low], axis=0)
            s_ref[:, pl.ds(pl.multiple_of(x * cells + pair * 128, 256), 256)] = both
            parts.append(both)
        both = jnp.concatenate(parts, axis=1)
        acc[...] += lax.dot_general(both, both, (((1,), (1,)), ((), ())), preferred_element_type=F32)

    @pl.loop(2, planes - 2, step=2)
    def _(x):
        plane(x, 0, True)
        plane(x + 1, 1, True)

    for copy in copies[0:2]:
        copy.wait()
    plane(0, 0, False)
    plane(1, 1, False)
    for copy in copies[2:4]:
        copy.wait()
    plane(planes - 2, 0, False)
    plane(planes - 1, 1, False)

    total = acc[0:32, :] + acc[32:64, :]
    gram = total[:, :32] + total[:, 32:]
    one[me] = jnp.concatenate([gram[8 * q:8 * q + 8, :] for q in range(4)], axis=1)

    def exchange(buf, mine, number, peer_of, send, recv):
        moves = []
        for k in range(1, number):
            copy = pltpu.make_async_remote_copy(
                src_ref=buf.at[mine], dst_ref=buf.at[mine], send_sem=send.at[k], recv_sem=recv.at[k],
                device_id=peer_of(k), device_id_type=MESH)
            copy.start()
            moves.append(copy)
        for copy in moves:
            copy.wait()
        total = buf[0]
        for k in range(1, number):
            total = total + buf[k]
        return total

    two[i_z] = exchange(one, me, count, plane_peer, send1, recv1)
    t_ref[...] = exchange(two, i_z, n_z, depth_peer, send2, recv2)


def factor(gram):
    lane = lax.broadcasted_iota(jnp.int32, (32, 128), 1)
    row = lax.broadcasted_iota(jnp.int32, (32, 128), 0)
    work = jnp.where(lane < 32, gram, jnp.where(lane - 32 == row, 1.0, 0.0))
    scale = jnp.zeros((32, 128), F32)
    for base in range(0, 32, 8):
        cols = [jnp.broadcast_to(work[:, base + q:base + q + 1], (32, 128)) for q in range(8)]
        for q in range(8):
            j = base + q
            pivot = jnp.broadcast_to(cols[q][j:j + 1, :], (32, 128))
            ratio = jnp.where(row > j, cols[q] * (1.0 / pivot), 0.0)
            for t in range(q + 1, 8):
                cols[t] = cols[t] - ratio * cols[t][j:j + 1, :]
            work = work - ratio * work[j:j + 1, :]
            scale = jnp.where(row == j, pivot, scale)
    return pltpu.roll(work, 96, 1) * lax.rsqrt(scale)


def basis_kernel(cells, planes, t_ref, s_ref, o_ref, stage, sems):
    width = s_ref.shape[1] // planes
    packed = t_ref[...] * (1.0 / cells)
    gram = jnp.concatenate([packed if q == 0 else pltpu.roll(packed, 128 - 32 * q, 1) for q in range(4)], axis=0)
    inverse = factor(gram)[:, :32]
    high, low = split(inverse)
    left = jnp.concatenate(
        [jnp.concatenate([high, high], axis=1), jnp.concatenate([low, low], axis=1)], axis=0)
    rows = o_ref.shape[2]
    flat = stage.reshape(32 * planes * rows, 128)
    copies = []
    for x in range(planes):
        wide = jnp.dot(left, s_ref[:, x * width:(x + 1) * width], preferred_element_type=F32)
        block = wide[:32] + wide[32:]
        for y in range(rows):
            flat[pl.ds(x * rows + y, 32, stride=planes * rows), :] = block[:, 128 * y:128 * y + 128]
        copy = pltpu.make_async_copy(stage.at[:, pl.ds(x * rows, rows), :], o_ref.at[:, x], sems.at[x])
        copy.start()
        copies.append(copy)
    for copy in copies:
        copy.wait()


def body(sizes, forward, adjoint, weights):
    _, planes, rows, depth = forward.shape
    half = 3 * planes
    plane_count = sizes[0] * sizes[1]
    cells = planes * rows * depth * plane_count * sizes[2]
    total, snaps = pl.pallas_call(
        functools.partial(snap_kernel, sizes),
        out_shape=(
            jax.ShapeDtypeStruct((64, planes * rows * depth), BF16),
            jax.ShapeDtypeStruct((8, 128), F32)),
        in_specs=[HBM] * 3,
        out_specs=(VMEM, VMEM),
        scratch_shapes=[
            pltpu.VMEM((6, planes + 4, rows, depth), F32),
            pltpu.VMEM((2 * half, rows + 16, depth), F32),
            pltpu.VMEM((2, 2, 2 * half, depth), F32),
            pltpu.VMEM((2, 2, rows, depth), F32),
            pltpu.VMEM((2, 2, 2 * half, depth), F32),
            pltpu.VMEM((2, 2, rows, depth), F32),
            pltpu.VMEM((32, 81), F32),
            pltpu.VMEM((2, rows * 32, depth), F32),
            pltpu.VMEM((2 * half, rows, depth), F32),
            pltpu.VMEM((2 * half, rows, depth), F32),
            pltpu.VMEM((64, 176), BF16),
            pltpu.VMEM((64, 64), F32),
            pltpu.VMEM((plane_count, 8, 128), F32),
            pltpu.VMEM((sizes[2], 8, 128), F32),
            pltpu.SemaphoreType.DMA((9,)),
            pltpu.SemaphoreType.DMA((8,)),
            pltpu.SemaphoreType.DMA((8,)),
            pltpu.SemaphoreType.DMA((plane_count,)),
            pltpu.SemaphoreType.DMA((plane_count,)),
            pltpu.SemaphoreType.DMA((sizes[2],)),
            pltpu.SemaphoreType.DMA((sizes[2],))],
        compiler_params=pltpu.CompilerParams(collective_id=0, has_side_effects=True, vmem_limit_bytes=LIMIT),
        name="snap",
    )(*[pltpu.with_memory_space_constraint(value, pltpu.HBM) for value in (forward, adjoint, weights)])[::-1]
    return pl.pallas_call(
        functools.partial(basis_kernel, cells, planes),
        out_shape=jax.ShapeDtypeStruct((32, planes, rows, depth), F32),
        in_specs=[VMEM, VMEM],
        out_specs=HBM,
        scratch_shapes=[
            pltpu.VMEM((32, planes * rows, depth), F32),
            pltpu.SemaphoreType.DMA((planes,))],
        compiler_params=pltpu.CompilerParams(vmem_limit_bytes=LIMIT),
        name="basis",
    )(total, snaps)


def solution(mesh):
    sizes = tuple(mesh.shape[name] for name in AXES)
    in_specs = (P(None, *AXES), P(None, *AXES), P())
    return jax.shard_map(
        functools.partial(body, sizes), mesh=mesh, in_specs=in_specs, out_specs=P(None, *AXES), check_vma=False)
```

```python
import functools

import jax
import jax.numpy as jnp
from jax import lax
from jax.experimental import pallas as pl
from jax.experimental.pallas import tpu as pltpu
from jax.sharding import PartitionSpec as P

MESH = pl.DeviceIdType.MESH
F32 = jnp.float32
BF16 = jnp.bfloat16
AXES = ("stream", "span", "depth")
HBM = pl.BlockSpec(memory_space=pltpu.HBM)
VMEM = pl.BlockSpec(memory_space=pltpu.VMEM)
LIMIT = 48 * 1024 * 1024


def split(value):
    high = value.astype(BF16)
    low = (value - high.astype(F32)).astype(BF16)
    return high, low


def snap_kernel(sizes, f_ref, a_ref, w_ref, s_ref, t_ref, px, py, hy, hz, ysend, zsend, wv, gs, sx, sz, lhs, acc,
                one, two, local, send, recv, send1, recv1, send2, recv2):
    n_s, n_y, n_z = sizes
    i_s, i_y, i_z = [lax.axis_index(name) for name in AXES]
    count = n_s * n_y
    me = i_s * n_y + i_y
    planes, rows = f_ref.shape[1], f_ref.shape[2]
    half = 3 * planes
    cells = rows * 128
    tall = rows + 16

    def plane_peer(k):
        other = lax.rem(me + k, count)
        return {"stream": other // n_y, "span": lax.rem(other, n_y)}

    def depth_peer(k):
        return {"depth": lax.rem(i_z + k, n_z)}

    barrier = pltpu.get_barrier_semaphore()
    for k in range(1, count):
        pl.semaphore_signal(barrier, inc=1, device_id=plane_peer(k), device_id_type=MESH)
    for k in range(1, n_z):
        pl.semaphore_signal(barrier, inc=1, device_id=depth_peer(k), device_id_type=MESH)

    loads = []

    def load(src, dst):
        copy = pltpu.make_async_copy(src, dst, local.at[len(loads)])
        copy.start()
        loads.append(copy)

    for k, ref in enumerate((f_ref, a_ref)):
        for c in range(3):
            m = 3 * k + c
            load(ref.at[c], py.at[m * planes:(m + 1) * planes, 8:8 + rows])
        load(ref, px.at[3 * k:3 * k + 3, 2:planes + 2])
    load(w_ref, wv)
    pl.semaphore_wait(barrier, count - 1 + n_z - 1)
    copies = []

    def push(src, dst, peer):
        n = len(copies)
        copy = pltpu.make_async_remote_copy(
            src_ref=src, dst_ref=dst, send_sem=send.at[n], recv_sem=recv.at[n],
            device_id=peer, device_id_type=MESH)
        copy.start()
        copies.append(copy)

    def sides(name, size, mine):
        return {name: lax.rem(mine + 1, size)}, {name: lax.rem(mine + size - 1, size)}

    after_x, before_x = sides("stream", n_s, i_s)
    after_y, before_y = sides("span", n_y, i_y)
    after_z, before_z = sides("depth", n_z, i_z)
    for k, ref in enumerate((f_ref, a_ref)):
        push(ref.at[:, planes - 2:planes], px.at[3 * k:3 * k + 3, 0:2], after_x)

    for copy in loads:
        copy.wait()
    flat = py.reshape(2 * half * tall, 128)
    for j in range(2):
        ysend[0, j] = flat[pl.ds(6 + rows + j, 2 * half, stride=tall), :]
        ysend[1, j] = flat[pl.ds(8 + j, 2 * half, stride=tall), :]
    lane = lax.broadcasted_iota(jnp.int32, (rows, 128), 1)
    for k in range(2):
        last = jnp.zeros((rows, 128), F32)
        first = jnp.zeros((rows, 128), F32)
        for i in range(half):
            own = py[k * half + i, 8:8 + rows, :]
            head = jnp.where(lane == 0, -own, 8.0 * pltpu.roll(own, 1, 1) - own)
            tail = jnp.where(lane == 126, own - 8.0 * pltpu.roll(own, 127, 1), own)
            head = pltpu.roll(head, 4 * i, 1) if i else head
            tail = pltpu.roll(tail, (4 * i + 4) % 128, 1)
            first = jnp.where(lane // 4 == i, head, first)
            last = jnp.where(lane // 4 == i, tail, last)
        zsend[0, k] = last
        zsend[1, k] = first

    push(ysend.at[0], hy.at[0], after_y)
    push(ysend.at[1], hy.at[1], before_y)
    push(zsend.at[0], hz.at[0], after_z)
    push(zsend.at[1], hz.at[1], before_z)
    for k, ref in enumerate((f_ref, a_ref)):
        push(ref.at[:, 0:2], px.at[3 * k:3 * k + 3, planes + 2:planes + 4], before_x)

    row = lax.broadcasted_iota(jnp.int32, (81, 176), 0)
    col = lax.broadcasted_iota(jnp.int32, (81, 176), 1)
    block, r = col // 16, col % 8
    source = jnp.where(block < 9, block * 9 + r, jnp.where(block == 9, r * 9 + 8, 80))
    keep = (row == source) & ((block < 10) | (r == 0))
    pick = jnp.where(keep, 1.0, 0.0).astype(BF16)
    w_high, w_low = split(wv[...] * (1.0 / 144.0))
    lhs[0:32, :] = jnp.dot(w_high, pick, preferred_element_type=F32).astype(BF16)
    lhs[32:64, :] = jnp.dot(w_low, pick, preferred_element_type=F32).astype(BF16)
    acc[...] = jnp.zeros_like(acc)

    def stencil(m2, m1, p1, p2):
        return 8.0 * (p1 - m1) - (p2 - m2)

    @pl.loop(0, planes)
    def _(x):
        for m in range(6):
            own = px[m, x + 2]
            p1 = jnp.where(lane == 127, 0.0, pltpu.roll(own, 127, 1))
            p2 = jnp.where(lane >= 126, 0.0, pltpu.roll(own, 126, 1))
            m1 = jnp.where(lane == 0, 0.0, pltpu.roll(own, 1, 1))
            m2 = jnp.where(lane <= 1, 0.0, pltpu.roll(own, 2, 1))
            sz[m * planes + x] = stencil(m2, m1, p1, p2)

    @pl.loop(2, planes - 2)
    def _(x):
        for m in range(6):
            sx[m * planes + x] = stencil(px[m, x], px[m, x + 1], px[m, x + 3], px[m, x + 4])

    for copy in copies[2:6]:
        copy.wait()
    for j in range(2):
        flat[pl.ds(6 + j, 2 * half, stride=tall), :] = hy[0, j]
        flat[pl.ds(8 + rows + j, 2 * half, stride=tall), :] = hy[1, j]

    def inner_x(x, k, c):
        m = 3 * k + c
        return stencil(px[m, x], px[m, x + 1], px[m, x + 3], px[m, x + 4])

    def plane(x, slot, ready):
        for k in range(2):
            halo_z = jnp.where(lane % 4 < 2, hz[1, k], hz[0, k])
            for c in range(3):
                i = (3 * k + c) * planes + x
                dx = sx[i] if ready else inner_x(x, k, c)
                dy = stencil(*[py[i, 8 + o:8 + o + rows, :] for o in (-2, -1, 1, 2)])
                edge = pltpu.roll(halo_z, lax.rem(254 - 4 * (c * planes + x), 128), 1)
                dz = sz[i] + jnp.where((lane < 2) | (lane >= 126), edge, 0.0)
                for d, slope in enumerate((dx, dy, dz)):
                    gs[slot, pl.ds(16 * k + 3 * c + d, rows, stride=32), :] = slope
        parts = []
        for pair in range(0, rows, 2):
            tiles = []
            for y in (pair, pair + 1):
                base = 32 * y
                f8 = gs[slot, base:base + 8, :]
                a8 = gs[slot, base + 16:base + 24, :]
                a_end = gs[slot, base + 24:base + 25, :]
                blocks = []
                for n in range(11):
                    if n < 9:
                        part = gs[slot, base + n:base + n + 1, :] * a8
                    elif n == 9:
                        part = f8 * a_end
                    else:
                        part = jnp.broadcast_to(gs[slot, base + 8:base + 9, :] * a_end, (8, 128))
                    high = part.astype(BF16).astype(F32)
                    blocks.append(jnp.concatenate([high, part - high], axis=0).astype(BF16))
                tiles.append(jnp.concatenate(blocks, axis=0))
            wide = jnp.dot(lhs[...], jnp.concatenate(tiles, axis=1), preferred_element_type=F32)
            high, low = split(wide[:32] + wide[32:])
            both = jnp.concatenate([high, low], axis=0)
            s_ref[:, pl.ds(pl.multiple_of(x * cells + pair * 128, 256), 256)] = both
            parts.append(both)
        both = jnp.concatenate(parts, axis=1)
        acc[...] += lax.dot_general(both, both, (((1,), (1,)), ((), ())), preferred_element_type=F32)

    @pl.loop(2, planes - 2, step=2)
    def _(x):
        plane(x, 0, True)
        plane(x + 1, 1, True)

    for copy in copies[0:2]:
        copy.wait()
    plane(0, 0, False)
    plane(1, 1, False)
    for copy in copies[6:8]:
        copy.wait()
    plane(planes - 2, 0, False)
    plane(planes - 1, 1, False)

    total = acc[0:32, :] + acc[32:64, :]
    gram = total[:, :32] + total[:, 32:]
    one[me] = jnp.concatenate([gram[8 * q:8 * q + 8, :] for q in range(4)], axis=1)

    def exchange(buf, mine, number, peer_of, send, recv):
        moves = []
        for k in range(1, number):
            copy = pltpu.make_async_remote_copy(
                src_ref=buf.at[mine], dst_ref=buf.at[mine], send_sem=send.at[k], recv_sem=recv.at[k],
                device_id=peer_of(k), device_id_type=MESH)
            copy.start()
            moves.append(copy)
        for copy in moves:
            copy.wait()
        total = buf[0]
        for k in range(1, number):
            total = total + buf[k]
        return total

    two[i_z] = exchange(one, me, count, plane_peer, send1, recv1)
    t_ref[...] = exchange(two, i_z, n_z, depth_peer, send2, recv2)


def factor(gram):
    lane = lax.broadcasted_iota(jnp.int32, (8, 128), 1)
    row = lax.broadcasted_iota(jnp.int32, (8, 128), 0)
    work = [
        jnp.where(lane < 32, gram[8 * b:8 * b + 8, :], jnp.where(lane - 32 == row + 8 * b, 1.0, 0.0))
        for b in range(4)]
    done = []
    for top in range(4):
        cols = [
            [jnp.broadcast_to(work[b][:, 8 * top + q:8 * top + q + 1], (8, 128)) for b in range(top, 4)]
            for q in range(8)]
        scale = jnp.zeros((8, 128), F32)
        for q in range(8):
            pivot = cols[q][0][q:q + 1, :]
            inverse = 1.0 / pivot
            scale = jnp.where(row == q, pivot, scale)
            heads = [cols[t][0][q:q + 1, :] for t in range(q + 1, 8)]
            lead = work[top][q:q + 1, :]
            for b in range(top, 4):
                ratio = cols[q][b - top] * inverse
                if b == top:
                    ratio = jnp.where(row > q, ratio, 0.0)
                for t, head in zip(range(q + 1, 8), heads):
                    cols[t][b - top] = cols[t][b - top] - ratio * head
                work[b] = work[b] - ratio * lead
        done.append(pltpu.roll(work[top], 96, 1) * lax.rsqrt(scale))
    return jnp.concatenate(done, axis=0)


def basis_kernel(cells, planes, t_ref, s_ref, o_ref, stage, sems):
    width = s_ref.shape[1] // planes
    packed = t_ref[...] * (1.0 / cells)
    gram = jnp.concatenate([packed if q == 0 else pltpu.roll(packed, 128 - 32 * q, 1) for q in range(4)], axis=0)
    inverse = factor(gram)[:, :32]
    high, low = split(inverse)
    left = jnp.concatenate(
        [jnp.concatenate([high, high], axis=1), jnp.concatenate([low, low], axis=1)], axis=0)
    rows = o_ref.shape[2]
    flat = stage.reshape(32 * planes * rows, 128)
    copies = []
    for x in range(planes):
        wide = jnp.dot(left, s_ref[:, x * width:(x + 1) * width], preferred_element_type=F32)
        block = wide[:32] + wide[32:]
        for y in range(rows):
            flat[pl.ds(x * rows + y, 32, stride=planes * rows), :] = block[:, 128 * y:128 * y + 128]
        copy = pltpu.make_async_copy(stage.at[:, pl.ds(x * rows, rows), :], o_ref.at[:, x], sems.at[x])
        copy.start()
        copies.append(copy)
    for copy in copies:
        copy.wait()


def body(sizes, forward, adjoint, weights):
    _, planes, rows, depth = forward.shape
    half = 3 * planes
    plane_count = sizes[0] * sizes[1]
    cells = planes * rows * depth * plane_count * sizes[2]
    total, snaps = pl.pallas_call(
        functools.partial(snap_kernel, sizes),
        out_shape=(
            jax.ShapeDtypeStruct((64, planes * rows * depth), BF16),
            jax.ShapeDtypeStruct((8, 128), F32)),
        in_specs=[HBM] * 3,
        out_specs=(VMEM, VMEM),
        scratch_shapes=[
            pltpu.VMEM((6, planes + 4, rows, depth), F32),
            pltpu.VMEM((2 * half, rows + 16, depth), F32),
            pltpu.VMEM((2, 2, 2 * half, depth), F32),
            pltpu.VMEM((2, 2, rows, depth), F32),
            pltpu.VMEM((2, 2, 2 * half, depth), F32),
            pltpu.VMEM((2, 2, rows, depth), F32),
            pltpu.VMEM((32, 81), F32),
            pltpu.VMEM((2, rows * 32, depth), F32),
            pltpu.VMEM((2 * half, rows, depth), F32),
            pltpu.VMEM((2 * half, rows, depth), F32),
            pltpu.VMEM((64, 176), BF16),
            pltpu.VMEM((64, 64), F32),
            pltpu.VMEM((plane_count, 8, 128), F32),
            pltpu.VMEM((sizes[2], 8, 128), F32),
            pltpu.SemaphoreType.DMA((9,)),
            pltpu.SemaphoreType.DMA((8,)),
            pltpu.SemaphoreType.DMA((8,)),
            pltpu.SemaphoreType.DMA((plane_count,)),
            pltpu.SemaphoreType.DMA((plane_count,)),
            pltpu.SemaphoreType.DMA((sizes[2],)),
            pltpu.SemaphoreType.DMA((sizes[2],))],
        compiler_params=pltpu.CompilerParams(collective_id=0, has_side_effects=True, vmem_limit_bytes=LIMIT),
        name="snap",
    )(*[pltpu.with_memory_space_constraint(value, pltpu.HBM) for value in (forward, adjoint, weights)])[::-1]
    return pl.pallas_call(
        functools.partial(basis_kernel, cells, planes),
        out_shape=jax.ShapeDtypeStruct((32, planes, rows, depth), F32),
        in_specs=[VMEM, VMEM],
        out_specs=HBM,
        scratch_shapes=[
            pltpu.VMEM((32, planes * rows, depth), F32),
            pltpu.SemaphoreType.DMA((planes,))],
        compiler_params=pltpu.CompilerParams(vmem_limit_bytes=LIMIT),
        name="basis",
    )(total, snaps)


def solution(mesh):
    sizes = tuple(mesh.shape[name] for name in AXES)
    in_specs = (P(None, *AXES), P(None, *AXES), P())
    return jax.shard_map(
        functools.partial(body, sizes), mesh=mesh, in_specs=in_specs, out_specs=P(None, *AXES), check_vma=False)
```

```python
import functools

import jax
import jax.numpy as jnp
from jax import lax
from jax.experimental import pallas as pl
from jax.experimental.pallas import tpu as pltpu
from jax.sharding import PartitionSpec as P

MESH = pl.DeviceIdType.MESH
F32 = jnp.float32
BF16 = jnp.bfloat16
AXES = ("stream", "span", "depth")
HBM = pl.BlockSpec(memory_space=pltpu.HBM)
VMEM = pl.BlockSpec(memory_space=pltpu.VMEM)
LIMIT = 48 * 1024 * 1024


def split(value):
    high = value.astype(BF16)
    low = (value - high.astype(F32)).astype(BF16)
    return high, low


def snap_kernel(sizes, f_ref, a_ref, w_ref, s_ref, t_ref, px, py, hy, hz, ysend, zsend, wv, gs, sx, sz, lhs, acc,
                one, two, local, send, recv, send1, recv1, send2, recv2):
    n_s, n_y, n_z = sizes
    i_s, i_y, i_z = [lax.axis_index(name) for name in AXES]
    count = n_s * n_y
    me = i_s * n_y + i_y
    planes, rows = f_ref.shape[1], f_ref.shape[2]
    half = 3 * planes
    cells = rows * 128
    tall = rows + 16

    def plane_peer(k):
        other = lax.rem(me + k, count)
        return {"stream": other // n_y, "span": lax.rem(other, n_y)}

    def depth_peer(k):
        return {"depth": lax.rem(i_z + k, n_z)}

    barrier = pltpu.get_barrier_semaphore()
    direct = count * n_z <= 32
    greeted = 0
    for z in range(n_z):
        for k in range(count):
            if (k or z) and (direct or not k or not z):
                peer = {**plane_peer(k), **depth_peer(z)}
                pl.semaphore_signal(barrier, inc=1, device_id=peer, device_id_type=MESH)
                greeted += 1

    loads = []

    def load(src, dst):
        copy = pltpu.make_async_copy(src, dst, local.at[len(loads)])
        copy.start()
        loads.append(copy)

    for k, ref in enumerate((f_ref, a_ref)):
        for c in range(3):
            m = 3 * k + c
            load(ref.at[c], py.at[m * planes:(m + 1) * planes, 8:8 + rows])
        load(ref, px.at[3 * k:3 * k + 3, 2:planes + 2])
    load(w_ref, wv)
    pl.semaphore_wait(barrier, greeted)
    copies = []

    def push(src, dst, peer):
        n = len(copies)
        copy = pltpu.make_async_remote_copy(
            src_ref=src, dst_ref=dst, send_sem=send.at[n], recv_sem=recv.at[n],
            device_id=peer, device_id_type=MESH)
        copy.start()
        copies.append(copy)

    def sides(name, size, mine):
        return {name: lax.rem(mine + 1, size)}, {name: lax.rem(mine + size - 1, size)}

    after_x, before_x = sides("stream", n_s, i_s)
    after_y, before_y = sides("span", n_y, i_y)
    after_z, before_z = sides("depth", n_z, i_z)
    for k, ref in enumerate((f_ref, a_ref)):
        push(ref.at[:, planes - 2:planes], px.at[3 * k:3 * k + 3, 0:2], after_x)

    for copy in loads:
        copy.wait()
    flat = py.reshape(2 * half * tall, 128)
    for j in range(2):
        ysend[0, j] = flat[pl.ds(6 + rows + j, 2 * half, stride=tall), :]
        ysend[1, j] = flat[pl.ds(8 + j, 2 * half, stride=tall), :]
    lane = lax.broadcasted_iota(jnp.int32, (rows, 128), 1)
    for k in range(2):
        last = jnp.zeros((rows, 128), F32)
        first = jnp.zeros((rows, 128), F32)
        for i in range(half):
            own = py[k * half + i, 8:8 + rows, :]
            head = jnp.where(lane == 0, -own, 8.0 * pltpu.roll(own, 1, 1) - own)
            tail = jnp.where(lane == 126, own - 8.0 * pltpu.roll(own, 127, 1), own)
            head = pltpu.roll(head, 4 * i, 1) if i else head
            tail = pltpu.roll(tail, (4 * i + 4) % 128, 1)
            first = jnp.where(lane // 4 == i, head, first)
            last = jnp.where(lane // 4 == i, tail, last)
        zsend[0, k] = last
        zsend[1, k] = first

    push(ysend.at[0], hy.at[0], after_y)
    push(ysend.at[1], hy.at[1], before_y)
    push(zsend.at[0], hz.at[0], after_z)
    push(zsend.at[1], hz.at[1], before_z)
    for k, ref in enumerate((f_ref, a_ref)):
        push(ref.at[:, 0:2], px.at[3 * k:3 * k + 3, planes + 2:planes + 4], before_x)

    row = lax.broadcasted_iota(jnp.int32, (81, 176), 0)
    col = lax.broadcasted_iota(jnp.int32, (81, 176), 1)
    block, r = col // 16, col % 8
    source = jnp.where(block < 9, block * 9 + r, jnp.where(block == 9, r * 9 + 8, 80))
    keep = (row == source) & ((block < 10) | (r == 0))
    pick = jnp.where(keep, 1.0, 0.0).astype(BF16)
    w_high, w_low = split(wv[...] * (1.0 / 144.0))
    lhs[0:32, :] = jnp.dot(w_high, pick, preferred_element_type=F32).astype(BF16)
    lhs[32:64, :] = jnp.dot(w_low, pick, preferred_element_type=F32).astype(BF16)
    acc[...] = jnp.zeros_like(acc)

    def stencil(m2, m1, p1, p2):
        return 8.0 * (p1 - m1) - (p2 - m2)

    @pl.loop(0, planes)
    def _(x):
        for m in range(6):
            own = px[m, x + 2]
            p1 = jnp.where(lane == 127, 0.0, pltpu.roll(own, 127, 1))
            p2 = jnp.where(lane >= 126, 0.0, pltpu.roll(own, 126, 1))
            m1 = jnp.where(lane == 0, 0.0, pltpu.roll(own, 1, 1))
            m2 = jnp.where(lane <= 1, 0.0, pltpu.roll(own, 2, 1))
            sz[m * planes + x] = stencil(m2, m1, p1, p2)

    @pl.loop(2, planes - 2)
    def _(x):
        for m in range(6):
            sx[m * planes + x] = stencil(px[m, x], px[m, x + 1], px[m, x + 3], px[m, x + 4])

    for copy in copies[2:6]:
        copy.wait()
    for j in range(2):
        flat[pl.ds(6 + j, 2 * half, stride=tall), :] = hy[0, j]
        flat[pl.ds(8 + rows + j, 2 * half, stride=tall), :] = hy[1, j]

    def inner_x(x, k, c):
        m = 3 * k + c
        return stencil(px[m, x], px[m, x + 1], px[m, x + 3], px[m, x + 4])

    def plane(x, slot, ready):
        for k in range(2):
            halo_z = jnp.where(lane % 4 < 2, hz[1, k], hz[0, k])
            for c in range(3):
                i = (3 * k + c) * planes + x
                dx = sx[i] if ready else inner_x(x, k, c)
                dy = stencil(*[py[i, 8 + o:8 + o + rows, :] for o in (-2, -1, 1, 2)])
                edge = pltpu.roll(halo_z, lax.rem(254 - 4 * (c * planes + x), 128), 1)
                dz = sz[i] + jnp.where((lane < 2) | (lane >= 126), edge, 0.0)
                for d, slope in enumerate((dx, dy, dz)):
                    gs[slot, pl.ds(16 * k + 3 * c + d, rows, stride=32), :] = slope
        parts = []
        for pair in range(0, rows, 2):
            tiles = []
            for y in (pair, pair + 1):
                base = 32 * y
                f8 = gs[slot, base:base + 8, :]
                a8 = gs[slot, base + 16:base + 24, :]
                a_end = gs[slot, base + 24:base + 25, :]
                blocks = []
                for n in range(11):
                    if n < 9:
                        part = gs[slot, base + n:base + n + 1, :] * a8
                    elif n == 9:
                        part = f8 * a_end
                    else:
                        part = jnp.broadcast_to(gs[slot, base + 8:base + 9, :] * a_end, (8, 128))
                    high = part.astype(BF16).astype(F32)
                    blocks.append(jnp.concatenate([high, part - high], axis=0).astype(BF16))
                tiles.append(jnp.concatenate(blocks, axis=0))
            wide = jnp.dot(lhs[...], jnp.concatenate(tiles, axis=1), preferred_element_type=F32)
            high, low = split(wide[:32] + wide[32:])
            both = jnp.concatenate([high, low], axis=0)
            s_ref[:, pl.ds(pl.multiple_of(x * cells + pair * 128, 256), 256)] = both
            parts.append(both)
        both = jnp.concatenate(parts, axis=1)
        acc[...] += lax.dot_general(both, both, (((1,), (1,)), ((), ())), preferred_element_type=F32)

    @pl.loop(2, planes - 2, step=2)
    def _(x):
        plane(x, 0, True)
        plane(x + 1, 1, True)

    for copy in copies[0:2]:
        copy.wait()
    plane(0, 0, False)
    plane(1, 1, False)
    for copy in copies[6:8]:
        copy.wait()
    plane(planes - 2, 0, False)
    plane(planes - 1, 1, False)

    total = acc[0:32, :] + acc[32:64, :]
    gram = total[:, :32] + total[:, 32:]
    packed = jnp.concatenate([gram[8 * q:8 * q + 8, :] for q in range(4)], axis=1)

    def exchange(buf, mine, number, peer_of, send, recv):
        moves = []
        for k in range(1, number):
            copy = pltpu.make_async_remote_copy(
                src_ref=buf.at[mine], dst_ref=buf.at[mine], send_sem=send.at[k], recv_sem=recv.at[k],
                device_id=peer_of(k), device_id_type=MESH)
            copy.start()
            moves.append(copy)
        for copy in moves:
            copy.wait()
        total = buf[0]
        for k in range(1, number):
            total = total + buf[k]
        return total

    if not direct:
        one[me] = packed
        two[i_z] = exchange(one, me, count, plane_peer, send1, recv1)
        t_ref[...] = exchange(two, i_z, n_z, depth_peer, send2, recv2)
        return
    everyone = me * n_z + i_z
    one[everyone] = packed
    moves = []
    for z in (*range(1, n_z), 0):
        for k in range(count - 1, -1, -1):
            if k == 0 and z == 0:
                continue
            slot = z * count + k
            copy = pltpu.make_async_remote_copy(
                src_ref=one.at[everyone], dst_ref=one.at[everyone], send_sem=send1.at[slot],
                recv_sem=recv1.at[slot], device_id={**plane_peer(k), **depth_peer(z)}, device_id_type=MESH)
            copy.start()
            moves.append(copy)
    for copy in moves:
        copy.wait()
    sums = [one[k] for k in range(count * n_z)]
    while len(sums) > 1:
        sums = [x + y for x, y in zip(sums[::2], sums[1::2])] + sums[len(sums) - len(sums) % 2:]
    t_ref[...] = sums[0]


def factor(gram):
    lane = lax.broadcasted_iota(jnp.int32, (8, 128), 1)
    row = lax.broadcasted_iota(jnp.int32, (8, 128), 0)
    work = [
        jnp.where(lane < 32, gram[8 * b:8 * b + 8, :], jnp.where(lane - 32 == row + 8 * b, 1.0, 0.0))
        for b in range(4)]
    done = []
    for top in range(4):
        cols = [
            [jnp.broadcast_to(work[b][:, 8 * top + q:8 * top + q + 1], (8, 128)) for b in range(top, 4)]
            for q in range(8)]
        scale = jnp.zeros((8, 128), F32)
        for q in range(8):
            pivot = cols[q][0][q:q + 1, :]
            inverse = 1.0 / pivot
            scale = jnp.where(row == q, pivot, scale)
            heads = [cols[t][0][q:q + 1, :] for t in range(q + 1, 8)]
            lead = work[top][q:q + 1, :]
            for b in range(top, 4):
                ratio = cols[q][b - top] * inverse
                if b == top:
                    ratio = jnp.where(row > q, ratio, 0.0)
                for t, head in zip(range(q + 1, 8), heads):
                    cols[t][b - top] = cols[t][b - top] - ratio * head
                work[b] = work[b] - ratio * lead
        done.append(pltpu.roll(work[top], 96, 1) * lax.rsqrt(scale))
    return jnp.concatenate(done, axis=0)


def basis_kernel(cells, planes, t_ref, s_ref, o_ref, stage, sems):
    width = s_ref.shape[1] // planes
    packed = t_ref[...] * (1.0 / cells)
    gram = jnp.concatenate([packed if q == 0 else pltpu.roll(packed, 128 - 32 * q, 1) for q in range(4)], axis=0)
    inverse = factor(gram)[:, :32]
    high, low = split(inverse)
    left = jnp.concatenate(
        [jnp.concatenate([high, high], axis=1), jnp.concatenate([low, low], axis=1)], axis=0)
    rows = o_ref.shape[2]
    flat = stage.reshape(32 * planes * rows, 128)
    copies = []
    for x in range(planes):
        wide = jnp.dot(left, s_ref[:, x * width:(x + 1) * width], preferred_element_type=F32)
        block = wide[:32] + wide[32:]
        for y in range(rows):
            flat[pl.ds(x * rows + y, 32, stride=planes * rows), :] = block[:, 128 * y:128 * y + 128]
        copy = pltpu.make_async_copy(stage.at[:, pl.ds(x * rows, rows), :], o_ref.at[:, x], sems.at[x])
        copy.start(priority=x % 2)
        copies.append(copy)
    for copy in copies:
        copy.wait()


def body(sizes, forward, adjoint, weights):
    _, planes, rows, depth = forward.shape
    half = 3 * planes
    plane_count = sizes[0] * sizes[1]
    slots = plane_count * sizes[2] if plane_count * sizes[2] <= 32 else plane_count
    cells = planes * rows * depth * plane_count * sizes[2]
    total, snaps = pl.pallas_call(
        functools.partial(snap_kernel, sizes),
        out_shape=(
            jax.ShapeDtypeStruct((64, planes * rows * depth), BF16),
            jax.ShapeDtypeStruct((8, 128), F32)),
        in_specs=[HBM] * 3,
        out_specs=(VMEM, VMEM),
        scratch_shapes=[
            pltpu.VMEM((6, planes + 4, rows, depth), F32),
            pltpu.VMEM((2 * half, rows + 16, depth), F32),
            pltpu.VMEM((2, 2, 2 * half, depth), F32),
            pltpu.VMEM((2, 2, rows, depth), F32),
            pltpu.VMEM((2, 2, 2 * half, depth), F32),
            pltpu.VMEM((2, 2, rows, depth), F32),
            pltpu.VMEM((32, 81), F32),
            pltpu.VMEM((2, rows * 32, depth), F32),
            pltpu.VMEM((2 * half, rows, depth), F32),
            pltpu.VMEM((2 * half, rows, depth), F32),
            pltpu.VMEM((64, 176), BF16),
            pltpu.VMEM((64, 64), F32),
            pltpu.VMEM((slots, 8, 128), F32),
            pltpu.VMEM((sizes[2], 8, 128), F32),
            pltpu.SemaphoreType.DMA((9,)),
            pltpu.SemaphoreType.DMA((8,)),
            pltpu.SemaphoreType.DMA((8,)),
            pltpu.SemaphoreType.DMA((slots,)),
            pltpu.SemaphoreType.DMA((slots,)),
            pltpu.SemaphoreType.DMA((sizes[2],)),
            pltpu.SemaphoreType.DMA((sizes[2],))],
        compiler_params=pltpu.CompilerParams(collective_id=0, has_side_effects=True, vmem_limit_bytes=LIMIT),
        name="snap",
    )(*[pltpu.with_memory_space_constraint(value, pltpu.HBM) for value in (forward, adjoint, weights)])[::-1]
    return pl.pallas_call(
        functools.partial(basis_kernel, cells, planes),
        out_shape=jax.ShapeDtypeStruct((32, planes, rows, depth), F32),
        in_specs=[VMEM, VMEM],
        out_specs=HBM,
        scratch_shapes=[
            pltpu.VMEM((32, planes * rows, depth), F32),
            pltpu.SemaphoreType.DMA((planes,))],
        compiler_params=pltpu.CompilerParams(vmem_limit_bytes=LIMIT),
        name="basis",
    )(total, snaps)


def solution(mesh):
    sizes = tuple(mesh.shape[name] for name in AXES)
    in_specs = (P(None, *AXES), P(None, *AXES), P())
    return jax.shard_map(
        functools.partial(body, sizes), mesh=mesh, in_specs=in_specs, out_specs=P(None, *AXES), check_vma=False)
```

```python
import functools

import jax
import jax.numpy as jnp
from jax import lax
from jax.experimental import pallas as pl
from jax.experimental.pallas import tpu as pltpu
from jax.sharding import PartitionSpec as P

MESH = pl.DeviceIdType.MESH
F32 = jnp.float32
BF16 = jnp.bfloat16
AXES = ("stream", "span", "depth")
HBM = pl.BlockSpec(memory_space=pltpu.HBM)
VMEM = pl.BlockSpec(memory_space=pltpu.VMEM)
LIMIT = 48 * 1024 * 1024


def split(value):
    high = value.astype(BF16)
    low = (value - high.astype(F32)).astype(BF16)
    return high, low


def snap_kernel(sizes, f_ref, a_ref, w_ref, s_ref, t_ref, px, py, hy, hz, ysend, zsend, wv, gs, sx, sz, lhs, acc,
                one, two, relay, local, send, recv, send1, recv1, send2, recv2):
    n_s, n_y, n_z = sizes
    i_s, i_y, i_z = [lax.axis_index(name) for name in AXES]
    count = n_s * n_y
    me = i_s * n_y + i_y
    planes, rows = f_ref.shape[1], f_ref.shape[2]
    half = 3 * planes
    cells = rows * 128
    tall = rows + 16

    def plane_peer(k):
        other = lax.rem(me + k, count)
        return {"stream": other // n_y, "span": lax.rem(other, n_y)}

    def depth_peer(k):
        return {"depth": lax.rem(i_z + k, n_z)}

    barrier = pltpu.get_barrier_semaphore()
    direct = count * n_z <= 32
    greeted = 0
    for z in range(n_z):
        for k in range(count):
            if (k or z) and (not k or not z):
                peer = {**plane_peer(k), **depth_peer(z)}
                pl.semaphore_signal(barrier, inc=1, device_id=peer, device_id_type=MESH)
                greeted += 1

    loads = []

    def load(src, dst):
        copy = pltpu.make_async_copy(src, dst, local.at[len(loads)])
        copy.start()
        loads.append(copy)

    for k, ref in enumerate((f_ref, a_ref)):
        for c in range(3):
            m = 3 * k + c
            load(ref.at[c], py.at[m * planes:(m + 1) * planes, 8:8 + rows])
        load(ref, px.at[3 * k:3 * k + 3, 2:planes + 2])
    load(w_ref, wv)
    pl.semaphore_wait(barrier, greeted)
    for k in range(1, n_z):
        pl.semaphore_signal(relay, inc=1, device_id=depth_peer(k), device_id_type=MESH)
    copies = []

    def push(src, dst, peer):
        n = len(copies)
        copy = pltpu.make_async_remote_copy(
            src_ref=src, dst_ref=dst, send_sem=send.at[n], recv_sem=recv.at[n],
            device_id=peer, device_id_type=MESH)
        copy.start()
        copies.append(copy)

    def sides(name, size, mine):
        return {name: lax.rem(mine + 1, size)}, {name: lax.rem(mine + size - 1, size)}

    after_x, before_x = sides("stream", n_s, i_s)
    after_y, before_y = sides("span", n_y, i_y)
    after_z, before_z = sides("depth", n_z, i_z)
    for k, ref in enumerate((f_ref, a_ref)):
        push(ref.at[:, planes - 2:planes], px.at[3 * k:3 * k + 3, 0:2], after_x)

    for copy in loads:
        copy.wait()
    flat = py.reshape(2 * half * tall, 128)
    for j in range(2):
        ysend[0, j] = flat[pl.ds(6 + rows + j, 2 * half, stride=tall), :]
        ysend[1, j] = flat[pl.ds(8 + j, 2 * half, stride=tall), :]
    lane = lax.broadcasted_iota(jnp.int32, (rows, 128), 1)
    for k in range(2):
        last = jnp.zeros((rows, 128), F32)
        first = jnp.zeros((rows, 128), F32)
        for i in range(half):
            own = py[k * half + i, 8:8 + rows, :]
            head = jnp.where(lane == 0, -own, 8.0 * pltpu.roll(own, 1, 1) - own)
            tail = jnp.where(lane == 126, own - 8.0 * pltpu.roll(own, 127, 1), own)
            head = pltpu.roll(head, 4 * i, 1) if i else head
            tail = pltpu.roll(tail, (4 * i + 4) % 128, 1)
            first = jnp.where(lane // 4 == i, head, first)
            last = jnp.where(lane // 4 == i, tail, last)
        zsend[0, k] = last
        zsend[1, k] = first

    push(ysend.at[0], hy.at[0], after_y)
    push(ysend.at[1], hy.at[1], before_y)
    push(zsend.at[0], hz.at[0], after_z)
    push(zsend.at[1], hz.at[1], before_z)
    for k, ref in enumerate((f_ref, a_ref)):
        push(ref.at[:, 0:2], px.at[3 * k:3 * k + 3, planes + 2:planes + 4], before_x)

    row = lax.broadcasted_iota(jnp.int32, (81, 176), 0)
    col = lax.broadcasted_iota(jnp.int32, (81, 176), 1)
    block, r = col // 16, col % 8
    source = jnp.where(block < 9, block * 9 + r, jnp.where(block == 9, r * 9 + 8, 80))
    keep = (row == source) & ((block < 10) | (r == 0))
    pick = jnp.where(keep, 1.0, 0.0).astype(BF16)
    w_high, w_low = split(wv[...] * (1.0 / 144.0))
    lhs[0:32, :] = jnp.dot(w_high, pick, preferred_element_type=F32).astype(BF16)
    lhs[32:64, :] = jnp.dot(w_low, pick, preferred_element_type=F32).astype(BF16)
    acc[...] = jnp.zeros_like(acc)

    def stencil(m2, m1, p1, p2):
        return 8.0 * (p1 - m1) - (p2 - m2)

    @pl.loop(0, planes)
    def _(x):
        for m in range(6):
            own = px[m, x + 2]
            p1 = jnp.where(lane == 127, 0.0, pltpu.roll(own, 127, 1))
            p2 = jnp.where(lane >= 126, 0.0, pltpu.roll(own, 126, 1))
            m1 = jnp.where(lane == 0, 0.0, pltpu.roll(own, 1, 1))
            m2 = jnp.where(lane <= 1, 0.0, pltpu.roll(own, 2, 1))
            sz[m * planes + x] = stencil(m2, m1, p1, p2)

    @pl.loop(2, planes - 2)
    def _(x):
        for m in range(6):
            sx[m * planes + x] = stencil(px[m, x], px[m, x + 1], px[m, x + 3], px[m, x + 4])

    for copy in copies[2:6]:
        copy.wait()
    for j in range(2):
        flat[pl.ds(6 + j, 2 * half, stride=tall), :] = hy[0, j]
        flat[pl.ds(8 + rows + j, 2 * half, stride=tall), :] = hy[1, j]

    def inner_x(x, k, c):
        m = 3 * k + c
        return stencil(px[m, x], px[m, x + 1], px[m, x + 3], px[m, x + 4])

    def plane(x, slot, ready):
        for k in range(2):
            halo_z = jnp.where(lane % 4 < 2, hz[1, k], hz[0, k])
            for c in range(3):
                i = (3 * k + c) * planes + x
                dx = sx[i] if ready else inner_x(x, k, c)
                dy = stencil(*[py[i, 8 + o:8 + o + rows, :] for o in (-2, -1, 1, 2)])
                edge = pltpu.roll(halo_z, lax.rem(254 - 4 * (c * planes + x), 128), 1)
                dz = sz[i] + jnp.where((lane < 2) | (lane >= 126), edge, 0.0)
                for d, slope in enumerate((dx, dy, dz)):
                    gs[slot, pl.ds(16 * k + 3 * c + d, rows, stride=32), :] = slope
        parts = []
        for pair in range(0, rows, 2):
            tiles = []
            for y in (pair, pair + 1):
                base = 32 * y
                f8 = gs[slot, base:base + 8, :]
                a8 = gs[slot, base + 16:base + 24, :]
                a_end = gs[slot, base + 24:base + 25, :]
                blocks = []
                for n in range(11):
                    if n < 9:
                        part = gs[slot, base + n:base + n + 1, :] * a8
                    elif n == 9:
                        part = f8 * a_end
                    else:
                        part = jnp.broadcast_to(gs[slot, base + 8:base + 9, :] * a_end, (8, 128))
                    high = part.astype(BF16).astype(F32)
                    blocks.append(jnp.concatenate([high, part - high], axis=0).astype(BF16))
                tiles.append(jnp.concatenate(blocks, axis=0))
            wide = jnp.dot(lhs[...], jnp.concatenate(tiles, axis=1), preferred_element_type=F32)
            high, low = split(wide[:32] + wide[32:])
            both = jnp.concatenate([high, low], axis=0)
            s_ref[:, pl.ds(pl.multiple_of(x * cells + pair * 128, 256), 256)] = both
            parts.append(both)
        both = jnp.concatenate(parts, axis=1)
        acc[...] += lax.dot_general(both, both, (((1,), (1,)), ((), ())), preferred_element_type=F32)

    @pl.loop(2, planes - 2, step=2)
    def _(x):
        plane(x, 0, True)
        plane(x + 1, 1, True)

    for copy in copies[0:2]:
        copy.wait()
    plane(0, 0, False)
    plane(1, 1, False)
    for copy in copies[6:8]:
        copy.wait()
    plane(planes - 2, 0, False)
    plane(planes - 1, 1, False)

    total = acc[0:32, :] + acc[32:64, :]
    gram = total[:, :32] + total[:, 32:]
    packed = jnp.concatenate([gram[8 * q:8 * q + 8, :] for q in range(4)], axis=1)

    def exchange(buf, mine, number, peer_of, send, recv):
        moves = []
        for k in range(1, number):
            copy = pltpu.make_async_remote_copy(
                src_ref=buf.at[mine], dst_ref=buf.at[mine], send_sem=send.at[k], recv_sem=recv.at[k],
                device_id=peer_of(k), device_id_type=MESH)
            copy.start()
            moves.append(copy)
        for copy in moves:
            copy.wait()
        total = buf[0]
        for k in range(1, number):
            total = total + buf[k]
        return total

    pl.semaphore_wait(relay, n_z - 1)
    if not direct:
        one[me] = packed
        two[i_z] = exchange(one, me, count, plane_peer, send1, recv1)
        t_ref[...] = exchange(two, i_z, n_z, depth_peer, send2, recv2)
        return
    everyone = me * n_z + i_z
    one[everyone] = packed
    moves = []
    for z in (*range(1, n_z), 0):
        for k in range(count - 1, -1, -1):
            if k == 0 and z == 0:
                continue
            slot = z * count + k
            copy = pltpu.make_async_remote_copy(
                src_ref=one.at[everyone], dst_ref=one.at[everyone], send_sem=send1.at[slot],
                recv_sem=recv1.at[slot], device_id={**plane_peer(k), **depth_peer(z)}, device_id_type=MESH)
            copy.start()
            moves.append(copy)
    for copy in moves:
        copy.wait()
    sums = [one[k] for k in range(count * n_z)]
    while len(sums) > 1:
        sums = [x + y for x, y in zip(sums[::2], sums[1::2])] + sums[len(sums) - len(sums) % 2:]
    t_ref[...] = sums[0]


def factor(gram):
    lane = lax.broadcasted_iota(jnp.int32, (8, 128), 1)
    row = lax.broadcasted_iota(jnp.int32, (8, 128), 0)
    work = [
        jnp.where(lane < 32, gram[8 * b:8 * b + 8, :], jnp.where(lane - 32 == row + 8 * b, 1.0, 0.0))
        for b in range(4)]
    done = []
    for top in range(4):
        cols = [
            [jnp.broadcast_to(work[b][:, 8 * top + q:8 * top + q + 1], (8, 128)) for b in range(top, 4)]
            for q in range(8)]
        scale = jnp.zeros((8, 128), F32)
        for q in range(8):
            pivot = cols[q][0][q:q + 1, :]
            inverse = 1.0 / pivot
            scale = jnp.where(row == q, pivot, scale)
            heads = [cols[t][0][q:q + 1, :] for t in range(q + 1, 8)]
            lead = work[top][q:q + 1, :]
            for b in range(top, 4):
                ratio = cols[q][b - top] * inverse
                if b == top:
                    ratio = jnp.where(row > q, ratio, 0.0)
                for t, head in zip(range(q + 1, 8), heads):
                    cols[t][b - top] = cols[t][b - top] - ratio * head
                work[b] = work[b] - ratio * lead
        done.append(pltpu.roll(work[top], 96, 1) * lax.rsqrt(scale))
    return jnp.concatenate(done, axis=0)


def basis_kernel(cells, planes, t_ref, s_ref, o_ref, stage, sems):
    width = s_ref.shape[1] // planes
    packed = t_ref[...] * (1.0 / cells)
    gram = jnp.concatenate([packed if q == 0 else pltpu.roll(packed, 128 - 32 * q, 1) for q in range(4)], axis=0)
    inverse = factor(gram)[:, :32]
    high, low = split(inverse)
    left = jnp.concatenate(
        [jnp.concatenate([high, high], axis=1), jnp.concatenate([low, low], axis=1)], axis=0)
    rows = o_ref.shape[2]
    copies = []
    for x in range(planes):
        wide = jnp.dot(left, s_ref[:, x * width:(x + 1) * width], preferred_element_type=F32)
        block = wide[:32] + wide[32:]
        stage[:, x * rows:(x + 1) * rows, :] = block.reshape(32, rows, 128)
        copy = pltpu.make_async_copy(stage.at[:, pl.ds(x * rows, rows), :], o_ref.at[:, x], sems.at[x])
        copy.start(priority=x % 2)
        copies.append(copy)
    for copy in copies:
        copy.wait()


def body(sizes, forward, adjoint, weights):
    _, planes, rows, depth = forward.shape
    half = 3 * planes
    plane_count = sizes[0] * sizes[1]
    slots = plane_count * sizes[2] if plane_count * sizes[2] <= 32 else plane_count
    cells = planes * rows * depth * plane_count * sizes[2]
    total, snaps = pl.pallas_call(
        functools.partial(snap_kernel, sizes),
        out_shape=(
            jax.ShapeDtypeStruct((64, planes * rows * depth), BF16),
            jax.ShapeDtypeStruct((8, 128), F32)),
        in_specs=[HBM] * 3,
        out_specs=(VMEM, VMEM),
        scratch_shapes=[
            pltpu.VMEM((6, planes + 4, rows, depth), F32),
            pltpu.VMEM((2 * half, rows + 16, depth), F32),
            pltpu.VMEM((2, 2, 2 * half, depth), F32),
            pltpu.VMEM((2, 2, rows, depth), F32),
            pltpu.VMEM((2, 2, 2 * half, depth), F32),
            pltpu.VMEM((2, 2, rows, depth), F32),
            pltpu.VMEM((32, 81), F32),
            pltpu.VMEM((2, rows * 32, depth), F32),
            pltpu.VMEM((2 * half, rows, depth), F32),
            pltpu.VMEM((2 * half, rows, depth), F32),
            pltpu.VMEM((64, 176), BF16),
            pltpu.VMEM((64, 64), F32),
            pltpu.VMEM((slots, 8, 128), F32),
            pltpu.VMEM((sizes[2], 8, 128), F32),
            pltpu.SemaphoreType.REGULAR,
            pltpu.SemaphoreType.DMA((9,)),
            pltpu.SemaphoreType.DMA((8,)),
            pltpu.SemaphoreType.DMA((8,)),
            pltpu.SemaphoreType.DMA((slots,)),
            pltpu.SemaphoreType.DMA((slots,)),
            pltpu.SemaphoreType.DMA((sizes[2],)),
            pltpu.SemaphoreType.DMA((sizes[2],))],
        compiler_params=pltpu.CompilerParams(collective_id=0, has_side_effects=True, vmem_limit_bytes=LIMIT),
        name="snap",
    )(*[pltpu.with_memory_space_constraint(value, pltpu.HBM) for value in (forward, adjoint, weights)])[::-1]
    return pl.pallas_call(
        functools.partial(basis_kernel, cells, planes),
        out_shape=jax.ShapeDtypeStruct((32, planes, rows, depth), F32),
        in_specs=[VMEM, VMEM],
        out_specs=HBM,
        scratch_shapes=[
            pltpu.VMEM((32, planes * rows, depth), F32),
            pltpu.SemaphoreType.DMA((planes,))],
        compiler_params=pltpu.CompilerParams(vmem_limit_bytes=LIMIT),
        name="basis",
    )(total, snaps)


def solution(mesh):
    sizes = tuple(mesh.shape[name] for name in AXES)
    in_specs = (P(None, *AXES), P(None, *AXES), P())
    return jax.shard_map(
        functools.partial(body, sizes), mesh=mesh, in_specs=in_specs, out_specs=P(None, *AXES), check_vma=False)
```

```python
import functools

import jax
import jax.numpy as jnp
from jax import lax
from jax.experimental import pallas as pl
from jax.experimental.pallas import tpu as pltpu
from jax.sharding import PartitionSpec as P

MESH = pl.DeviceIdType.MESH
F32 = jnp.float32
BF16 = jnp.bfloat16
AXES = ("stream", "span", "depth")
HBM = pl.BlockSpec(memory_space=pltpu.HBM)
VMEM = pl.BlockSpec(memory_space=pltpu.VMEM)
LIMIT = 48 * 1024 * 1024


def split(value):
    high = value.astype(BF16)
    low = (value - high.astype(F32)).astype(BF16)
    return high, low


def snap_kernel(sizes, f_ref, a_ref, w_ref, s_ref, t_ref, px, py, hy, hz, ysend, zsend, wv, gs, sx, sz, lhs, acc,
                one, two, relay, local, send, recv, send1, recv1, send2, recv2):
    n_s, n_y, n_z = sizes
    i_s, i_y, i_z = [lax.axis_index(name) for name in AXES]
    count = n_s * n_y
    me = i_s * n_y + i_y
    planes, rows = f_ref.shape[1], f_ref.shape[2]
    half = 3 * planes
    cells = rows * 128
    tall = rows + 16

    def plane_peer(k):
        other = lax.rem(me + k, count)
        return {"stream": other // n_y, "span": lax.rem(other, n_y)}

    def depth_peer(k):
        return {"depth": lax.rem(i_z + k, n_z)}

    barrier = pltpu.get_barrier_semaphore()
    direct = count * n_z <= 32
    greeted = 0
    for z in range(n_z):
        for k in range(count):
            if (k or z) and (not k or not z):
                peer = {**plane_peer(k), **depth_peer(z)}
                pl.semaphore_signal(barrier, inc=1, device_id=peer, device_id_type=MESH)
                greeted += 1

    loads = []

    def load(src, dst):
        copy = pltpu.make_async_copy(src, dst, local.at[len(loads)])
        copy.start()
        loads.append(copy)

    for k, ref in enumerate((f_ref, a_ref)):
        for c in range(3):
            m = 3 * k + c
            load(ref.at[c], py.at[m * planes:(m + 1) * planes, 8:8 + rows])
        load(ref, px.at[3 * k:3 * k + 3, 2:planes + 2])
    load(w_ref, wv)
    pl.semaphore_wait(barrier, greeted)
    for k in range(1, n_z):
        pl.semaphore_signal(relay, inc=1, device_id=depth_peer(k), device_id_type=MESH)
    copies = []

    def push(src, dst, peer):
        n = len(copies)
        copy = pltpu.make_async_remote_copy(
            src_ref=src, dst_ref=dst, send_sem=send.at[n], recv_sem=recv.at[n],
            device_id=peer, device_id_type=MESH)
        copy.start()
        copies.append(copy)

    def sides(name, size, mine):
        return {name: lax.rem(mine + 1, size)}, {name: lax.rem(mine + size - 1, size)}

    after_x, before_x = sides("stream", n_s, i_s)
    after_y, before_y = sides("span", n_y, i_y)
    after_z, before_z = sides("depth", n_z, i_z)
    for k, ref in enumerate((f_ref, a_ref)):
        push(ref.at[:, planes - 2:planes], px.at[3 * k:3 * k + 3, 0:2], after_x)

    for copy in loads:
        copy.wait()
    flat = py.reshape(2 * half * tall, 128)
    for j in range(2):
        ysend[0, j] = flat[pl.ds(6 + rows + j, 2 * half, stride=tall), :]
        ysend[1, j] = flat[pl.ds(8 + j, 2 * half, stride=tall), :]
    lane = lax.broadcasted_iota(jnp.int32, (rows, 128), 1)
    for k in range(2):
        last = jnp.zeros((rows, 128), F32)
        first = jnp.zeros((rows, 128), F32)
        for i in range(half):
            own = py[k * half + i, 8:8 + rows, :]
            head = jnp.where(lane == 0, -own, 8.0 * pltpu.roll(own, 1, 1) - own)
            tail = jnp.where(lane == 126, own - 8.0 * pltpu.roll(own, 127, 1), own)
            head = pltpu.roll(head, 4 * i, 1) if i else head
            tail = pltpu.roll(tail, (4 * i + 4) % 128, 1)
            first = jnp.where(lane // 4 == i, head, first)
            last = jnp.where(lane // 4 == i, tail, last)
        zsend[0, k] = last
        zsend[1, k] = first

    push(ysend.at[0], hy.at[0], after_y)
    push(ysend.at[1], hy.at[1], before_y)
    push(zsend.at[0], hz.at[0], after_z)
    push(zsend.at[1], hz.at[1], before_z)
    for k, ref in enumerate((f_ref, a_ref)):
        push(ref.at[:, 0:2], px.at[3 * k:3 * k + 3, planes + 2:planes + 4], before_x)

    row = lax.broadcasted_iota(jnp.int32, (81, 176), 0)
    col = lax.broadcasted_iota(jnp.int32, (81, 176), 1)
    block, r = col // 16, col % 8
    source = jnp.where(block < 9, block * 9 + r, jnp.where(block == 9, r * 9 + 8, 80))
    keep = (row == source) & ((block < 10) | (r == 0))
    pick = jnp.where(keep, 1.0, 0.0).astype(BF16)
    w_high, w_low = split(wv[...] * (1.0 / 144.0))
    lhs[0:32, :] = jnp.dot(w_high, pick, preferred_element_type=F32).astype(BF16)
    lhs[32:64, :] = jnp.dot(w_low, pick, preferred_element_type=F32).astype(BF16)
    acc[...] = jnp.zeros_like(acc)

    def stencil(m2, m1, p1, p2):
        return 8.0 * (p1 - m1) - (p2 - m2)

    @pl.loop(0, planes)
    def _(x):
        for m in range(6):
            own = px[m, x + 2]
            p1 = jnp.where(lane == 127, 0.0, pltpu.roll(own, 127, 1))
            p2 = jnp.where(lane >= 126, 0.0, pltpu.roll(own, 126, 1))
            m1 = jnp.where(lane == 0, 0.0, pltpu.roll(own, 1, 1))
            m2 = jnp.where(lane <= 1, 0.0, pltpu.roll(own, 2, 1))
            sz[m * planes + x] = stencil(m2, m1, p1, p2)

    @pl.loop(2, planes - 2)
    def _(x):
        for m in range(6):
            sx[m * planes + x] = stencil(px[m, x], px[m, x + 1], px[m, x + 3], px[m, x + 4])

    for copy in copies[2:6]:
        copy.wait()
    for j in range(2):
        flat[pl.ds(6 + j, 2 * half, stride=tall), :] = hy[0, j]
        flat[pl.ds(8 + rows + j, 2 * half, stride=tall), :] = hy[1, j]

    def inner_x(x, k, c):
        m = 3 * k + c
        return stencil(px[m, x], px[m, x + 1], px[m, x + 3], px[m, x + 4])

    def plane(x, slot, ready):
        for k in range(2):
            slopes = []
            halo_z = jnp.where(lane % 4 < 2, hz[1, k], hz[0, k])
            for c in range(3):
                i = (3 * k + c) * planes + x
                dx = sx[i] if ready else inner_x(x, k, c)
                dy = stencil(*[py[i, 8 + o:8 + o + rows, :] for o in (-2, -1, 1, 2)])
                edge = pltpu.roll(halo_z, lax.rem(254 - 4 * (c * planes + x), 128), 1)
                dz = sz[i] + jnp.where((lane < 2) | (lane >= 126), edge, 0.0)
                slopes += [dx, dy, dz]
            gs[slot, 16 * k:16 * k + 8, :] = jnp.stack(slopes[:8]).reshape(8, cells)
            gs[slot, 16 * k + 8:16 * k + 9, :] = slopes[8].reshape(1, cells)
        parts = []
        for pair in range(0, rows, 2):
            tiles = []
            for y in (pair, pair + 1):
                at = slice(128 * y, 128 * y + 128)
                f8 = gs[slot, 0:8, at]
                a8 = gs[slot, 16:24, at]
                a_end = gs[slot, 24:25, at]
                blocks = []
                for n in range(11):
                    if n < 9:
                        part = gs[slot, n:n + 1, at] * a8
                    elif n == 9:
                        part = f8 * a_end
                    else:
                        part = jnp.broadcast_to(gs[slot, 8:9, at] * a_end, (8, 128))
                    high = part.astype(BF16).astype(F32)
                    blocks.append(jnp.concatenate([high, part - high], axis=0).astype(BF16))
                tiles.append(jnp.concatenate(blocks, axis=0))
            wide = jnp.dot(lhs[...], jnp.concatenate(tiles, axis=1), preferred_element_type=F32)
            high, low = split(wide[:32] + wide[32:])
            both = jnp.concatenate([high, low], axis=0)
            s_ref[:, pl.ds(pl.multiple_of(x * cells + pair * 128, 256), 256)] = both
            parts.append(both)
        both = jnp.concatenate(parts, axis=1)
        acc[...] += lax.dot_general(both, both, (((1,), (1,)), ((), ())), preferred_element_type=F32)

    @pl.loop(2, planes - 2, step=2)
    def _(x):
        plane(x, 0, True)
        plane(x + 1, 1, True)

    for copy in copies[0:2]:
        copy.wait()
    plane(0, 0, False)
    plane(1, 1, False)
    for copy in copies[6:8]:
        copy.wait()
    plane(planes - 2, 0, False)
    plane(planes - 1, 1, False)

    total = acc[0:32, :] + acc[32:64, :]
    gram = total[:, :32] + total[:, 32:]
    packed = jnp.concatenate([gram[8 * q:8 * q + 8, :] for q in range(4)], axis=1)

    def exchange(buf, mine, number, peer_of, send, recv):
        moves = []
        for k in range(1, number):
            copy = pltpu.make_async_remote_copy(
                src_ref=buf.at[mine], dst_ref=buf.at[mine], send_sem=send.at[k], recv_sem=recv.at[k],
                device_id=peer_of(k), device_id_type=MESH)
            copy.start()
            moves.append(copy)
        for copy in moves:
            copy.wait()
        total = buf[0]
        for k in range(1, number):
            total = total + buf[k]
        return total

    pl.semaphore_wait(relay, n_z - 1)
    if not direct:
        one[me] = packed
        two[i_z] = exchange(one, me, count, plane_peer, send1, recv1)
        t_ref[...] = exchange(two, i_z, n_z, depth_peer, send2, recv2)
        return
    everyone = me * n_z + i_z
    one[everyone] = packed
    moves = []
    for z in (*range(1, n_z), 0):
        for k in range(count - 1, -1, -1):
            if k == 0 and z == 0:
                continue
            slot = z * count + k
            copy = pltpu.make_async_remote_copy(
                src_ref=one.at[everyone], dst_ref=one.at[everyone], send_sem=send1.at[slot],
                recv_sem=recv1.at[slot], device_id={**plane_peer(k), **depth_peer(z)}, device_id_type=MESH)
            copy.start()
            moves.append(copy)
    for copy in moves:
        copy.wait()
    sums = [one[k] for k in range(count * n_z)]
    while len(sums) > 1:
        sums = [x + y for x, y in zip(sums[::2], sums[1::2])] + sums[len(sums) - len(sums) % 2:]
    t_ref[...] = sums[0]


def factor(gram):
    lane = lax.broadcasted_iota(jnp.int32, (8, 128), 1)
    row = lax.broadcasted_iota(jnp.int32, (8, 128), 0)
    work = [
        jnp.where(lane < 32, gram[8 * b:8 * b + 8, :], jnp.where(lane - 32 == row + 8 * b, 1.0, 0.0))
        for b in range(4)]
    done = []
    for top in range(4):
        cols = [
            [jnp.broadcast_to(work[b][:, 8 * top + q:8 * top + q + 1], (8, 128)) for b in range(top, 4)]
            for q in range(8)]
        scale = jnp.zeros((8, 128), F32)
        for q in range(8):
            pivot = cols[q][0][q:q + 1, :]
            inverse = 1.0 / pivot
            scale = jnp.where(row == q, pivot, scale)
            heads = [cols[t][0][q:q + 1, :] for t in range(q + 1, 8)]
            lead = work[top][q:q + 1, :]
            for b in range(top, 4):
                ratio = cols[q][b - top] * inverse
                if b == top:
                    ratio = jnp.where(row > q, ratio, 0.0)
                for t, head in zip(range(q + 1, 8), heads):
                    cols[t][b - top] = cols[t][b - top] - ratio * head
                work[b] = work[b] - ratio * lead
        done.append(pltpu.roll(work[top], 96, 1) * lax.rsqrt(scale))
    return jnp.concatenate(done, axis=0)


def basis_kernel(cells, planes, t_ref, s_ref, o_ref, stage, sems):
    width = s_ref.shape[1] // planes
    packed = t_ref[...] * (1.0 / cells)
    gram = jnp.concatenate([packed if q == 0 else pltpu.roll(packed, 128 - 32 * q, 1) for q in range(4)], axis=0)
    inverse = factor(gram)[:, :32]
    high, low = split(inverse)
    left = jnp.concatenate(
        [jnp.concatenate([high, high], axis=1), jnp.concatenate([low, low], axis=1)], axis=0)
    rows = o_ref.shape[2]
    copies = []
    for x in range(planes):
        wide = jnp.dot(left, s_ref[:, x * width:(x + 1) * width], preferred_element_type=F32)
        block = wide[:32] + wide[32:]
        stage[:, x * rows:(x + 1) * rows, :] = block.reshape(32, rows, 128)
        copy = pltpu.make_async_copy(stage.at[:, pl.ds(x * rows, rows), :], o_ref.at[:, x], sems.at[x])
        copy.start(priority=x % 2)
        copies.append(copy)
    for copy in copies:
        copy.wait()


def body(sizes, forward, adjoint, weights):
    _, planes, rows, depth = forward.shape
    half = 3 * planes
    plane_count = sizes[0] * sizes[1]
    slots = plane_count * sizes[2] if plane_count * sizes[2] <= 32 else plane_count
    cells = planes * rows * depth * plane_count * sizes[2]
    total, snaps = pl.pallas_call(
        functools.partial(snap_kernel, sizes),
        out_shape=(
            jax.ShapeDtypeStruct((64, planes * rows * depth), BF16),
            jax.ShapeDtypeStruct((8, 128), F32)),
        in_specs=[HBM] * 3,
        out_specs=(VMEM, VMEM),
        scratch_shapes=[
            pltpu.VMEM((6, planes + 4, rows, depth), F32),
            pltpu.VMEM((2 * half, rows + 16, depth), F32),
            pltpu.VMEM((2, 2, 2 * half, depth), F32),
            pltpu.VMEM((2, 2, rows, depth), F32),
            pltpu.VMEM((2, 2, 2 * half, depth), F32),
            pltpu.VMEM((2, 2, rows, depth), F32),
            pltpu.VMEM((32, 81), F32),
            pltpu.VMEM((2, 32, rows * depth), F32),
            pltpu.VMEM((2 * half, rows, depth), F32),
            pltpu.VMEM((2 * half, rows, depth), F32),
            pltpu.VMEM((64, 176), BF16),
            pltpu.VMEM((64, 64), F32),
            pltpu.VMEM((slots, 8, 128), F32),
            pltpu.VMEM((sizes[2], 8, 128), F32),
            pltpu.SemaphoreType.REGULAR,
            pltpu.SemaphoreType.DMA((9,)),
            pltpu.SemaphoreType.DMA((8,)),
            pltpu.SemaphoreType.DMA((8,)),
            pltpu.SemaphoreType.DMA((slots,)),
            pltpu.SemaphoreType.DMA((slots,)),
            pltpu.SemaphoreType.DMA((sizes[2],)),
            pltpu.SemaphoreType.DMA((sizes[2],))],
        compiler_params=pltpu.CompilerParams(collective_id=0, has_side_effects=True, vmem_limit_bytes=LIMIT),
        name="snap",
    )(*[pltpu.with_memory_space_constraint(value, pltpu.HBM) for value in (forward, adjoint, weights)])[::-1]
    return pl.pallas_call(
        functools.partial(basis_kernel, cells, planes),
        out_shape=jax.ShapeDtypeStruct((32, planes, rows, depth), F32),
        in_specs=[VMEM, VMEM],
        out_specs=HBM,
        scratch_shapes=[
            pltpu.VMEM((32, planes * rows, depth), F32),
            pltpu.SemaphoreType.DMA((planes,))],
        compiler_params=pltpu.CompilerParams(vmem_limit_bytes=LIMIT),
        name="basis",
    )(total, snaps)


def solution(mesh):
    sizes = tuple(mesh.shape[name] for name in AXES)
    in_specs = (P(None, *AXES), P(None, *AXES), P())
    return jax.shard_map(
        functools.partial(body, sizes), mesh=mesh, in_specs=in_specs, out_specs=P(None, *AXES), check_vma=False)
```
